256 devices in a mesh: row: 16 (over x_hi, y, core), col: 8 (over z), depth: 2 (over x_lo).
Axes of the slice: x: 4 (x_hi: 2, x_lo: 2; x = x_hi * 2 + x_lo), y: 4, z: 8, core: 2. Of those that a mesh axis runs over, the one named last changes fastest.
Arguments:
- slab_adj: float32 [65536, 8192], P('row', ('col', 'depth')), may hold values from -6 to 6
- panel_rows: float32 [65536, 256], P(('row', 'col', 'depth')), may hold values from -0.0234375 to 0.0234375
- panel_cols: float32 [8192, 256], P(('col', 'depth')), may hold values from -0.0625 to 0.0625
- bar_rows: float32 [65536, 256], P(('row', 'col', 'depth')), may hold values from -6 to 6
- bar_cols: float32 [8192, 256], P(('col', 'depth')), may hold values from -6 to 6
- inv_diag: float32 [256, 256], replicated, may hold values from -1 to 2, as said below
- bar_diag: float32 [256, 256], replicated, may hold values from -6 to 6
Outputs:
- adj_rows: float32 [65536, 256], P(('row', 'col', 'depth'))
- adj_cols: float32 [8192, 256], P(('col', 'depth'))
- diag_adj: float32 [256, 256], replicated
The draws below stay inside these ranges and needn't reach their ends.
Inputs may be any that keep to these rules, and one draw needn't show every extreme that they name: `inv_diag`: lower triangular; diagonal entries between 1 and 2.
All inputs are finite; a program needn't handle non-finite values.
Results may differ from the reference program's by a relative error of at most 0.00007.
Values sent between devices are 32-bit elements; how exact they have to be, the bound alone decides.
No kernel may reach another device: no remote copies, remote signals or barrier semaphores. Data moves between devices by JAX's collectives and lax.ppermute only.
A program may use at most 64 MiB of HBM per device.

```python
import jax
import jax.numpy as jnp
from jax import lax

NB = 256
M = 65536
C = 8192


def draw_inv_diag(key, part):
    key = jax.random.fold_in(key, 11)
    first, second = jax.random.split(key)
    diag_vals = jax.random.uniform(first, (NB,), jnp.float32, 1.0, 2.0)
    lower = jnp.clip(jax.random.normal(second, (NB, NB), jnp.float32), -2.5, 2.5) * (0.6 / NB ** 0.5)
    return jnp.tril(lower, -1) + jnp.diag(diag_vals)


def block_levels(key, dims, cuts, low, high):
    def one(axis_at, blocks):
        draws = jax.random.uniform(jax.random.fold_in(jax.random.fold_in(key, 6), axis_at), (blocks,), jnp.float32, low / len(cuts), high / len(cuts))
        return jnp.repeat(jnp.exp(draws), dims[axis_at] // blocks).reshape((-1,) + (1,) * (len(dims) - axis_at - 1))

    level = one(*cuts[0])
    for cut in cuts[1:]:
        level = level * one(*cut)
    return level


def gaussian(own_key, dims, width, bound, shards=(), held_as=jnp.bfloat16):
    array = jax.random.normal(own_key, dims, jnp.float32) * width
    if len(shards) > 0:
        array = block_levels(own_key, dims, shards, -0.22, 0.18) * array
    return jnp.clip(array, min=-bound, max=bound).astype(held_as)


def setup_inputs(seed: int = 0) -> dict:
    arg_keys = jax.random.split(jax.random.key(seed), 8)
    return {
        "slab_adj": gaussian(arg_keys[0], (M, C), 1.0, 6.0, ((0, 16), (1, 16)), jnp.float32),
        "panel_rows": gaussian(arg_keys[1], (M, NB), M ** -0.5, 0.0234375, ((0, 256),), jnp.float32),
        "panel_cols": gaussian(arg_keys[2], (C, NB), C ** -0.5, 0.0625, ((0, 16),), jnp.float32),
        "bar_rows": gaussian(arg_keys[3], (M, NB), 1.0, 6.0, ((0, 256),), jnp.float32),
        "bar_cols": gaussian(arg_keys[4], (C, NB), 1.0, 6.0, ((0, 16),), jnp.float32),
        "inv_diag": draw_inv_diag(jax.random.fold_in(arg_keys[7], 71), 0),
        "bar_diag": gaussian(arg_keys[6], (NB, NB), 1.0, 6.0, (), jnp.float32),
    }


def reference(slab_adj, panel_rows, panel_cols, bar_rows, bar_cols, inv_diag, bar_diag):
    high = lax.Precision.HIGHEST
    term_rows = jnp.dot(slab_adj, panel_cols, precision=high, preferred_element_type=jnp.float32)
    term_cols = jnp.dot(slab_adj.T, panel_rows, precision=high, preferred_element_type=jnp.float32)
    adj_rows = jnp.dot(bar_rows - term_rows, inv_diag, precision=high, preferred_element_type=jnp.float32)
    adj_cols = jnp.dot(bar_cols - term_cols, inv_diag, precision=high, preferred_element_type=jnp.float32)
    diag_adj = bar_diag - jnp.dot(adj_rows.T, panel_rows, precision=high, preferred_element_type=jnp.float32)
    diag_adj = diag_adj - jnp.dot(adj_cols.T, panel_cols, precision=high, preferred_element_type=jnp.float32)
    return adj_rows, adj_cols, diag_adj
```

```python
import jax
import jax.numpy as jnp
from jax import lax
from jax.sharding import PartitionSpec as P

HIGH = lax.Precision.HIGH
F32 = jnp.float32


def dot(a, b):
    return jnp.dot(a, b, precision=HIGH, preferred_element_type=F32)


def dot_t(a, b):
    return lax.dot_general(a, b, (((0,), (0,)), ((), ())), precision=HIGH, preferred_element_type=F32)


def rows(a, start, size):
    return lax.dynamic_slice_in_dim(a, start, size, 0)


def z_shift(a, k):
    return lax.ppermute(a, "col", [(i, (i + k) % 8) for i in range(8)])


def z_xor(a, k):
    return lax.ppermute(a, "col", [(i, i ^ k) for i in range(8)])


def x_swap(a):
    return lax.ppermute(a, "depth", [(0, 1), (1, 0)])


def core_swap(a):
    return lax.ppermute(a, "row", [(i, i ^ 1) for i in range(16)])


def far_swap(a):
    return lax.ppermute(a, "row", [(i, i ^ 8) for i in range(16)])


def y_shift(a, k):
    return lax.ppermute(a, "row", [(i, (i & 9) | ((((i >> 1) + k) & 3) << 1)) for i in range(16)])


def body(slab_adj, panel_rows, panel_cols, bar_rows, bar_cols, inv_diag, bar_diag):
    r = lax.axis_index("row")
    c = lax.axis_index("col")
    d = lax.axis_index("depth")
    core, y, far = r & 1, (r >> 1) & 3, r >> 3

    other_b = x_swap(panel_rows[128:])
    other_a = x_swap(panel_rows[:128])
    right, left = [panel_rows], [panel_rows]
    right_b, left_b = [other_b], [other_b]
    over_x = [None]
    for k in range(1, 4):
        right.append(z_shift(right[-1], 1))
        left.append(z_shift(left[-1], -1))
        right_b.append(z_shift(right_b[-1], 1))
        left_b.append(z_shift(left_b[-1], -1))
        over_x.append(x_swap(jnp.concatenate([right[k][:128], left[k][:128]], 0)))
    right.append(z_shift(right[3][:128], 1))
    left.append(z_shift(left[3][128:], -1))
    right_b.append(z_shift(right_b[3][:64], 1))
    left_b.append(z_shift(left_b[3][64:], -1))
    over_x.append(x_swap(right[4]))

    def slab(cc, dd):
        return rows(slab_adj, ((cc & 7) * 2 + dd) * 256, 256)

    cat = lambda *a: jnp.concatenate(a, 0)
    e = 1 - d
    product = dot_t(slab(c, d), panel_rows) + dot_t(slab(c, e), cat(other_a, other_b))
    for k in range(1, 4):
        product = product + dot_t(slab(c - k, d), right[k]) + dot_t(slab(c + k, d), left[k])
        product = product + dot_t(slab(c - k, e), cat(over_x[k][:128], right_b[k]))
        product = product + dot_t(slab(c + k, e), cat(over_x[k][128:], left_b[k]))
    product = product + dot_t(slab(c + 4, d), cat(right[4], left[4]))
    product = product + dot_t(slab(c + 4, e), cat(over_x[4], right_b[4], left_b[4]))

    part = dot(slab_adj, panel_cols)
    part, _, _ = lax.optimization_barrier((part, right[3], left[3]))

    def piece(cc, dd):
        return rows(part, ((cc & 7) * 2 + dd) * 256, 256)

    to_r = z_shift(piece(c + 4, e), 1)
    to_l = z_shift(piece(c + 4, d), -1)
    r_e = z_shift(piece(c + 3, e) + to_r, 1)
    l_e = z_shift(piece(c - 3, e), -1)
    r_d = z_shift(piece(c + 3, d), 1)
    l_d = z_shift(piece(c - 3, d) + to_l, -1)
    for k in (2, 1):
        r_e = z_shift(piece(c + k, e) + r_e, 1)
        l_e = z_shift(piece(c - k, e) + l_e, -1)
        r_d = z_shift(piece(c + k, d) + r_d, 1)
        l_d = z_shift(piece(c - k, d) + l_d, -1)
    term_rows = (piece(c, d) + r_d + l_d) + x_swap(piece(c, e) + r_e + l_e)
    adj_rows = dot(bar_rows - term_rows, inv_diag)

    share = rows(bar_cols, r * 32, 32)
    share_cols = rows(panel_cols, r * 32, 32)
    ahead = dot_t(cat(bar_rows, share), cat(panel_rows, share_cols))
    both = ahead - dot_t(cat(panel_cols, product), cat(product, panel_cols))

    def half(cc):
        return cat(rows(product, cc * 256, 256), rows(both, cc * 128, 128))

    v = half(core) + core_swap(half(1 - core))

    def quarter(yy):
        yy = yy & 3
        return cat(rows(v, yy * 64, 64), rows(v, 256 + yy * 32, 32))

    v = (
        quarter(y)
        + y_shift(quarter(y + 1), 1)
        + y_shift(quarter(y - 1), -1)
        + y_shift(quarter(y + 2), 2)
    )

    def eighth(ff):
        return cat(rows(v, ff * 32, 32), rows(v, 64 + ff * 16, 16))

    v = eighth(far) + far_swap(eighth(1 - far))
    t = v[32:]
    t = t + x_swap(t)
    for k in (1, 2, 4):
        t = t + z_xor(t, k)
    v = cat(v[:32], t)
    w = far_swap(v)
    first = far == 0
    v = jnp.where(first, v, w), jnp.where(first, w, v)
    v = cat(v[0][:32], v[1][:32], v[0][32:], v[1][32:])
    p1, m1, p2 = y_shift(v, -1), y_shift(v, 1), y_shift(v, 2)
    ring = cat(v, p1, p2, m1, v, p1, p2)
    ring = rows(ring, ((4 - y) & 3) * 96, 384).reshape(4, 96, 256)
    v = cat(ring[:, :64].reshape(256, 256), ring[:, 64:].reshape(128, 256))
    w = core_swap(v)
    first = core == 0
    lo, hi = jnp.where(first, v, w), jnp.where(first, w, v)
    term_cols = cat(lo[:256], hi[:256])
    total = cat(lo[256:], hi[256:])
    adj_cols = dot(bar_cols - term_cols, inv_diag)
    diag_adj = bar_diag - dot_t(inv_diag, total)
    return adj_rows, adj_cols, diag_adj


def solution(mesh):
    in_specs = (
        P("row", ("col", "depth")),
        P(("row", "col", "depth"), None),
        P(("col", "depth"), None),
        P(("row", "col", "depth"), None),
        P(("col", "depth"), None),
        P(),
        P(),
    )
    out_specs = (P(("row", "col", "depth"), None), P(("col", "depth"), None), P())
    return jax.shard_map(body, mesh=mesh, in_specs=in_specs, out_specs=out_specs, check_vma=False)
```

```python
import jax
import jax.numpy as jnp
from jax import lax
from jax.sharding import PartitionSpec as P

HIGH = lax.Precision.HIGH
F32 = jnp.float32


def dot(a, b):
    return jnp.dot(a, b, precision=HIGH, preferred_element_type=F32)


def dot_t(a, b):
    return lax.dot_general(a, b, (((0,), (0,)), ((), ())), precision=HIGH, preferred_element_type=F32)


def rows(a, start, size):
    return lax.dynamic_slice_in_dim(a, start, size, 0)


def z_shift(a, k):
    return lax.ppermute(a, "col", [(i, (i + k) % 8) for i in range(8)])


def z_xor(a, k):
    return lax.ppermute(a, "col", [(i, i ^ k) for i in range(8)])


def x_swap(a):
    return lax.ppermute(a, "depth", [(0, 1), (1, 0)])


def core_swap(a):
    return lax.ppermute(a, "row", [(i, i ^ 1) for i in range(16)])


def far_swap(a):
    return lax.ppermute(a, "row", [(i, i ^ 8) for i in range(16)])


def y_shift(a, k):
    return lax.ppermute(a, "row", [(i, (i & 9) | ((((i >> 1) + k) & 3) << 1)) for i in range(16)])


def body(slab_adj, panel_rows, panel_cols, bar_rows, bar_cols, inv_diag, bar_diag):
    r = lax.axis_index("row")
    c = lax.axis_index("col")
    d = lax.axis_index("depth")
    core, y, far = r & 1, (r >> 1) & 3, r >> 3

    cat = lambda *a: jnp.concatenate(a, 0)
    hold = lax.optimization_barrier
    e = 1 - d

    def slab(cc, dd):
        return rows(slab_adj, ((cc & 7) * 2 + dd) * 256, 256)

    own = panel_rows
    right, left, other = z_shift(own, 1), z_shift(own, -1), x_swap(own)
    part = dot(slab_adj, panel_cols)
    share = rows(bar_cols, r * 32, 32)
    share_cols = rows(panel_cols, r * 32, 32)
    ahead = dot_t(cat(bar_rows, share), cat(panel_rows, share_cols))
    right, left, other, part, ahead = hold((right, left, other, part, ahead))
    term_rows = lax.psum_scatter(part, ("col", "depth"), scatter_dimension=0, tiled=True)

    product = dot_t(slab(c, d), own) + dot_t(slab(c, e), other)
    product = product + dot_t(slab(c - 1, d), right) + dot_t(slab(c + 1, d), left)
    over_x = x_swap(cat(right[:128], left[:128]))
    right = z_shift(cat(right, other[128:]), 1)
    left = z_shift(cat(other[128:], left), -1)
    right, left, over_x, product = hold((right, left, over_x, product))

    def add_far(product, k, right, left):
        product = product + dot_t(slab(c - k, d), right[:256])
        return product + dot_t(slab(c + k, d), left[128:])

    def add_other(product, k, over_x, right_b, left_b):
        product = product + dot_t(slab(c - k, e), cat(over_x[:128], right_b))
        return product + dot_t(slab(c + k, e), cat(over_x[128:], left_b))

    product = add_far(product, 2, right, left)
    product = add_other(product, 1, over_x, right[256:], left[:128])
    over_x = x_swap(cat(right[:128], left[128:256]))
    right, left = z_shift(right, 1), z_shift(left, -1)
    right, left, over_x, product = hold((right, left, over_x, product))

    product = add_far(product, 3, right, left)
    product = add_other(product, 2, over_x, right[256:], left[:128])
    over_x = x_swap(cat(right[:128], left[128:256]))
    right, left = z_shift(right[128:], 1), z_shift(left[:256], -1)
    right, left, over_x, product = hold((right, left, over_x, product))

    far_own = cat(left[128:], right[:128])
    product = product + dot_t(slab(c + 4, d), far_own)
    product = add_other(product, 3, over_x, right[128:], left[:128])
    over_x = x_swap(far_own)
    over_x, product = hold((over_x, product))
    product = product + dot_t(slab(c + 4, e), over_x)

    adj_rows = dot(bar_rows - term_rows, inv_diag)

    both = ahead - dot_t(cat(panel_cols, product), cat(product, panel_cols))

    def half(cc):
        return cat(rows(product, cc * 256, 256), rows(both, cc * 128, 128))

    v = half(core) + core_swap(half(1 - core))

    def quarter(yy):
        yy = yy & 3
        return cat(rows(v, yy * 64, 64), rows(v, 256 + yy * 32, 32))

    v = (
        quarter(y)
        + y_shift(quarter(y + 1), 1)
        + y_shift(quarter(y - 1), -1)
        + y_shift(quarter(y + 2), 2)
    )

    def eighth(ff):
        return cat(rows(v, ff * 32, 32), rows(v, 64 + ff * 16, 16))

    v = eighth(far) + far_swap(eighth(1 - far))
    t = v[32:]
    t = t + x_swap(t)
    for k in (1, 2, 4):
        t = t + z_xor(t, k)
    v = cat(v[:32], t)
    w = far_swap(v)
    first = far == 0
    v = jnp.where(first, v, w), jnp.where(first, w, v)
    v = cat(v[0][:32], v[1][:32], v[0][32:], v[1][32:])
    p1, m1, p2 = y_shift(v, -1), y_shift(v, 1), y_shift(v, 2)
    ring = cat(v, p1, p2, m1, v, p1, p2)
    ring = rows(ring, ((4 - y) & 3) * 96, 384).reshape(4, 96, 256)
    v = cat(ring[:, :64].reshape(256, 256), ring[:, 64:].reshape(128, 256))
    w = core_swap(v)
    first = core == 0
    lo, hi = jnp.where(first, v, w), jnp.where(first, w, v)
    term_cols = cat(lo[:256], hi[:256])
    total = cat(lo[256:], hi[256:])
    adj_cols = dot(bar_cols - term_cols, inv_diag)
    diag_adj = bar_diag - dot_t(inv_diag, total)
    return adj_rows, adj_cols, diag_adj


def solution(mesh):
    in_specs = (
        P("row", ("col", "depth")),
        P(("row", "col", "depth"), None),
        P(("col", "depth"), None),
        P(("row", "col", "depth"), None),
        P(("col", "depth"), None),
        P(),
        P(),
    )
    out_specs = (P(("row", "col", "depth"), None), P(("col", "depth"), None), P())
    return jax.shard_map(body, mesh=mesh, in_specs=in_specs, out_specs=out_specs, check_vma=False)
```

```python
import jax
import jax.numpy as jnp
from jax import lax
from jax.sharding import PartitionSpec as P

HIGH = lax.Precision.HIGH
F32 = jnp.float32


def dot(a, b):
    return jnp.dot(a, b, precision=HIGH, preferred_element_type=F32)


def dot_t(a, b):
    return lax.dot_general(a, b, (((0,), (0,)), ((), ())), precision=HIGH, preferred_element_type=F32)


def rows(a, start, size):
    return lax.dynamic_slice_in_dim(a, start, size, 0)


def z_shift(a, k):
    return lax.ppermute(a, "col", [(i, (i + k) % 8) for i in range(8)])


def z_xor(a, k):
    return lax.ppermute(a, "col", [(i, i ^ k) for i in range(8)])


def x_swap(a):
    return lax.ppermute(a, "depth", [(0, 1), (1, 0)])


def core_swap(a):
    return lax.ppermute(a, "row", [(i, i ^ 1) for i in range(16)])


def far_swap(a):
    return lax.ppermute(a, "row", [(i, i ^ 8) for i in range(16)])


def diagonal_swap(a):
    return lax.ppermute(a, ("row", "depth"), [(i, i ^ 17) for i in range(32)])


def y_shift(a, k):
    return lax.ppermute(a, "row", [(i, (i & 9) | ((((i >> 1) + k) & 3) << 1)) for i in range(16)])


def body(slab_adj, panel_rows, panel_cols, bar_rows, bar_cols, inv_diag, bar_diag):
    r = lax.axis_index("row")
    c = lax.axis_index("col")
    d = lax.axis_index("depth")
    core, y, far = r & 1, (r >> 1) & 3, r >> 3

    cat = lambda *a: jnp.concatenate(a, 0)
    hold = lax.optimization_barrier
    e = 1 - d

    def slab(cc, dd):
        return rows(slab_adj, ((cc & 7) * 2 + dd) * 256, 256)

    def add(product, blk, cc, dd):
        return product + dot_t(slab(cc, dd), blk)

    def part(cc, cols):
        return dot(rows(slab_adj, (cc & 7) * 512, 512), cols)

    own = panel_rows
    right, left, other = z_shift(own, 1), z_shift(own, -1), x_swap(own)
    product = dot_t(slab(c, d), own)
    part_4 = part(c + 4, panel_cols)
    share = rows(bar_cols, r * 32, 32)
    share_cols = rows(panel_cols, r * 32, 32)
    ahead = dot_t(cat(bar_rows, share), cat(panel_rows, share_cols))
    right, left, other, part_4, ahead, product, cols = hold((right, left, other, part_4, ahead, product, panel_cols))

    over_x = x_swap(cat(right[:128], left[:128]))
    to_right, to_left = z_shift(cat(right, other[128:]), 1), z_shift(cat(other[128:], left), -1)
    product = add(product, other, c, e)
    product = add(product, right, c - 1, d)
    product = add(product, left, c + 1, d)
    part_r3 = part(c + 3, cols)
    right, left, over_x, product, part_r3, cols = hold((to_right, to_left, over_x, product, part_r3, cols))

    def add_other(product, k, over_x, right_b, left_b):
        product = add(product, cat(over_x[:128], right_b), c - k, e)
        return add(product, cat(over_x[128:], left_b), c + k, e)

    next_x = x_swap(cat(right[:128], left[128:256]))
    to_right, to_left = z_shift(right, 1), z_shift(left, -1)
    product = add(product, right[:256], c - 2, d)
    product = add(product, left[128:], c + 2, d)
    product = add_other(product, 1, over_x, right[256:], left[:128])
    part_l3 = part(c - 3, cols)
    right, left, over_x, product, part_l3, cols = hold((to_right, to_left, next_x, product, part_l3, cols))

    next_x = x_swap(cat(right[:128], left[128:256]))
    to_right, to_left = z_shift(right[128:], 1), z_shift(left[:256], -1)
    product = add(product, right[:256], c - 3, d)
    product = add(product, left[128:], c + 3, d)
    product = add_other(product, 2, over_x, right[256:], left[:128])
    part_r2 = part(c + 2, cols)
    right, left, over_x, product, part_r2, part_4, cols = hold(
        (to_right, to_left, next_x, product, part_r2, part_4, cols)
    )

    far_own = cat(left[128:], right[:128])
    next_x = x_swap(far_own)
    to_right, to_left = z_shift(part_4[:256], 1), z_shift(part_4[256:], -1)
    product = add(product, far_own, c + 4, d)
    product = add_other(product, 3, over_x, right[128:], left[:128])
    part_l2 = part(c - 2, cols)
    right, left, over_x, product, part_l2, cols = hold((to_right, to_left, next_x, product, part_l2, cols))
    right = z_shift(cat(part_r3[:256] + right, part_r3[256:]), 1)
    left = z_shift(cat(part_l3[:256], part_l3[256:] + left), -1)
    product = add(product, over_x, c + 4, e)

    both = ahead - dot_t(cat(panel_cols, product), cat(product, panel_cols))

    def half(cc):
        return cat(rows(product, cc * 256, 256), rows(both, cc * 128, 128))

    v = half(core) + core_swap(half(1 - core))

    def quarter(yy):
        yy = yy & 3
        return cat(rows(v, yy * 64, 64), rows(v, 256 + yy * 32, 32))

    v = (
        quarter(y)
        + y_shift(quarter(y + 1), 1)
        + y_shift(quarter(y - 1), -1)
        + y_shift(quarter(y + 2), 2)
    )

    part_r1 = part(c + 1, cols)
    v, right, left, part_r1, cols = hold((v, right, left, part_r1, cols))
    right, left = z_shift(part_r2 + right, 1), z_shift(part_l2 + left, -1)
    a, b, g = far_swap(v), x_swap(v[64:]), diagonal_swap(v[64:])
    t = (v[64:] + b) + (a[64:] + g)
    t = t + z_xor(t, 1)
    part_l1 = part(c - 1, cols)
    t, right, left, part_l1, cols = hold((t, right, left, part_l1, cols))
    right, left = z_shift(part_r1 + right, 1), z_shift(part_l1 + left, -1)
    t = (t + z_xor(t, 2)) + (z_xor(t, 4) + z_xor(t, 6))
    v = cat(v[:64] + a[:64], t)
    part_0 = part(c, cols)
    v, part_0 = hold((v, part_0))
    p1, m1, p2 = y_shift(v, -1), y_shift(v, 1), y_shift(v, 2)
    ring = cat(v, p1, p2, m1, v, p1, p2)
    ring = rows(ring, ((4 - y) & 3) * 96, 384).reshape(4, 96, 256)
    v = cat(ring[:, :64].reshape(256, 256), ring[:, 64:].reshape(128, 256))
    v, right, left = hold((v, right, left))
    whole = part_0 + right + left
    over_x = x_swap(rows(whole, e * 256, 256))
    w = core_swap(v)
    first = core == 0
    lo, hi = jnp.where(first, v, w), jnp.where(first, w, v)
    term_cols = cat(lo[:256], hi[:256])
    total = cat(lo[256:], hi[256:])
    term_rows = rows(whole, d * 256, 256) + over_x
    adj_rows = dot(bar_rows - term_rows, inv_diag)
    adj_cols = dot(bar_cols - term_cols, inv_diag)
    diag_adj = bar_diag - dot_t(inv_diag, total)
    return adj_rows, adj_cols, diag_adj


def solution(mesh):
    in_specs = (
        P("row", ("col", "depth")),
        P(("row", "col", "depth"), None),
        P(("col", "depth"), None),
        P(("row", "col", "depth"), None),
        P(("col", "depth"), None),
        P(),
        P(),
    )
    out_specs = (P(("row", "col", "depth"), None), P(("col", "depth"), None), P())
    return jax.shard_map(body, mesh=mesh, in_specs=in_specs, out_specs=out_specs, check_vma=False)
```

```python
import jax
import jax.numpy as jnp
from jax import lax
from jax.sharding import PartitionSpec as P

HIGH = lax.Precision.HIGH
F32 = jnp.float32


def dot(a, b):
    return jnp.dot(a, b, precision=HIGH, preferred_element_type=F32)


def dot_t(a, b):
    return lax.dot_general(a, b, (((0,), (0,)), ((), ())), precision=HIGH, preferred_element_type=F32)


def rows(a, start, size):
    return lax.dynamic_slice_in_dim(a, start, size, 0)


def z_shift(a, k):
    return lax.ppermute(a, "col", [(i, (i + k) % 8) for i in range(8)])


def z_xor(a, k):
    return lax.ppermute(a, "col", [(i, i ^ k) for i in range(8)])


def x_swap(a):
    return lax.ppermute(a, "depth", [(0, 1), (1, 0)])


def core_swap(a):
    return lax.ppermute(a, "row", [(i, i ^ 1) for i in range(16)])


def far_swap(a):
    return lax.ppermute(a, "row", [(i, i ^ 8) for i in range(16)])


def diagonal_swap(a):
    return lax.ppermute(a, ("row", "depth"), [(i, i ^ 17) for i in range(32)])


def y_shift(a, k):
    return lax.ppermute(a, "row", [(i, (i & 9) | ((((i >> 1) + k) & 3) << 1)) for i in range(16)])


def body(slab_adj, panel_rows, panel_cols, bar_rows, bar_cols, inv_diag, bar_diag):
    r = lax.axis_index("row")
    c = lax.axis_index("col")
    d = lax.axis_index("depth")
    core, y, far = r & 1, (r >> 1) & 3, r >> 3

    cat = lambda *a: jnp.concatenate(a, 0)
    hold = lax.optimization_barrier
    e = 1 - d

    def slab(cc, dd):
        return rows(slab_adj, ((cc & 7) * 2 + dd) * 256, 256)

    def add(product, blk, cc, dd):
        return product + dot_t(slab(cc, dd), blk)

    def part(cc, cols):
        return dot(rows(slab_adj, (cc & 7) * 512, 512), cols)

    own = panel_rows
    right, left, other = z_shift(own, 1), z_shift(own, -1), x_swap(own)
    other, own, inv = hold((other, own, inv_diag))
    product = dot_t(slab(c, d), own)
    inv_t = inv.T
    right, left, other, product, cols, inv_t = hold((right, left, other, product, panel_cols, inv_t))

    over_x = x_swap(cat(right[:128], left[:128]))
    to_right, to_left = z_shift(cat(right, other[128:]), 1), z_shift(cat(other[128:], left), -1)
    over_x, right, left, product, cols = hold((over_x, right, left, product, cols))
    product = add(product, other, c, e)
    product = add(product, right, c - 1, d)
    product = add(product, left, c + 1, d)
    part_4 = part(c + 4, cols)
    right, left, over_x, product, part_4, cols = hold((to_right, to_left, over_x, product, part_4, cols))

    def add_other(product, k, over_x, right_b, left_b):
        product = add(product, cat(over_x[:128], right_b), c - k, e)
        return add(product, cat(over_x[128:], left_b), c + k, e)

    next_x = x_swap(cat(right[:128], left[128:256]))
    to_right, to_left = z_shift(right, 1), z_shift(left, -1)
    next_x, right, left, product, cols = hold((next_x, right, left, product, cols))
    product = add(product, right[:256], c - 2, d)
    product = add(product, left[128:], c + 2, d)
    product = add_other(product, 1, over_x, right[256:], left[:128])
    part_r3, part_l3 = part(c + 3, cols), part(c - 3, cols)
    right, left, over_x, product, part_r3, part_l3, cols = hold(
        (to_right, to_left, next_x, product, part_r3, part_l3, cols)
    )

    next_x = x_swap(cat(right[:128], left[128:256]))
    to_right = z_shift(cat(right[128:], part_4[:256]), 1)
    to_left = z_shift(cat(left[:256], part_4[256:]), -1)
    next_x, right, left, product, cols = hold((next_x, right, left, product, cols))
    product = add(product, right[:256], c - 3, d)
    product = add(product, left[128:], c + 3, d)
    product = add_other(product, 2, over_x, right[256:], left[:128])
    part_r2, part_l2 = part(c + 2, cols), part(c - 2, cols)
    share = rows(bar_cols, r * 32, 32)
    share_cols = rows(cols, r * 32, 32)
    ahead = dot_t(cat(bar_rows, share), cat(panel_rows, share_cols))
    right, left, over_x, product, part_r2, part_l2, ahead, cols = hold(
        (to_right, to_left, next_x, product, part_r2, part_l2, ahead, cols)
    )

    far_own = cat(left[128:256], right[:128])
    next_x = x_swap(far_own)
    sum_r = z_shift(cat(part_r3[:256] + right[256:], part_r3[256:]), 1)
    sum_l = z_shift(cat(part_l3[:256], part_l3[256:] + left[256:]), -1)
    product = add(product, far_own, c + 4, d)
    product = add_other(product, 3, over_x, right[128:256], left[:128])
    over_x, product, cols = hold((next_x, product, cols))
    product = add(product, over_x, c + 4, e)

    both = ahead - dot_t(cat(panel_cols, product), cat(product, panel_cols))

    def half(cc):
        return cat(rows(product, cc * 256, 256), rows(both, cc * 128, 128))

    v, sum_r, sum_l, cols = hold((core_swap(half(1 - core)), sum_r, sum_l, cols))
    sum_r, sum_l = z_shift(part_r2 + sum_r, 1), z_shift(part_l2 + sum_l, -1)
    v = half(core) + v

    def quarter(yy):
        yy = yy & 3
        return cat(rows(v, yy * 64, 64), rows(v, 256 + yy * 32, 32))

    from_left, from_right, across = y_shift(quarter(y + 1), 1), y_shift(quarter(y - 1), -1), y_shift(quarter(y + 2), 2)
    part_r1, part_l1 = part(c + 1, cols), part(c - 1, cols)
    v = quarter(y) + from_left + from_right + across
    v, part_r1, part_l1, cols = hold((v, part_r1, part_l1, cols))
    a, b, g = far_swap(v), x_swap(v[64:]), diagonal_swap(v[64:])
    a, b, g, sum_r, sum_l = hold((a, b, g, sum_r, sum_l))
    t = (v[64:] + b) + (a[64:] + g)
    t = t + z_xor(t, 1)
    t, sum_r, sum_l, cols = hold((t, sum_r, sum_l, cols))
    sum_r, sum_l = z_shift(part_r1 + sum_r, 1), z_shift(part_l1 + sum_l, -1)
    part_0 = part(c, cols)
    t = (t + z_xor(t, 2)) + (z_xor(t, 4) + z_xor(t, 6))
    v = cat(v[:64] + a[:64], t)
    v, part_0 = hold((v, part_0))
    p1, m1, p2 = y_shift(v, -1), y_shift(v, 1), y_shift(v, 2)
    ring = cat(v, p1, p2, m1, v, p1, p2)
    ring = rows(ring, ((4 - y) & 3) * 96, 384).reshape(4, 96, 256)
    v = cat(ring[:, :64].reshape(256, 256), ring[:, 64:].reshape(128, 256))
    v, sum_r, sum_l = hold((v, sum_r, sum_l))
    whole = part_0 + sum_r + sum_l
    over_x = x_swap(rows(whole, e * 256, 256))
    w = core_swap(v)
    first = core == 0
    lo, hi = jnp.where(first, v, w), jnp.where(first, w, v)
    term_cols = cat(lo[:256], hi[:256])
    total = cat(lo[256:], hi[256:])
    term_rows = rows(whole, d * 256, 256) + over_x
    adj_rows = dot(bar_rows - term_rows, inv_diag)
    adj_cols = dot(bar_cols - term_cols, inv_diag)
    diag_adj = bar_diag - dot(inv_t, total)
    return adj_rows, adj_cols, diag_adj


def solution(mesh):
    in_specs = (
        P("row", ("col", "depth")),
        P(("row", "col", "depth"), None),
        P(("col", "depth"), None),
        P(("row", "col", "depth"), None),
        P(("col", "depth"), None),
        P(),
        P(),
    )
    out_specs = (P(("row", "col", "depth"), None), P(("col", "depth"), None), P())
    return jax.shard_map(body, mesh=mesh, in_specs=in_specs, out_specs=out_specs, check_vma=False)
```

```python
import functools

import jax
import jax.numpy as jnp
from jax import lax
from jax.experimental import pallas as pl
from jax.experimental.pallas import tpu as pltpu
from jax.sharding import PartitionSpec as P

HIGH = lax.Precision.HIGH
F32 = jnp.float32


def dot(a, b):
    return jnp.dot(a, b, precision=HIGH, preferred_element_type=F32)


def dot_t(a, b):
    return lax.dot_general(a, b, (((0,), (0,)), ((), ())), precision=HIGH, preferred_element_type=F32)


VMEM = pl.BlockSpec(memory_space=pltpu.VMEM)
SMEM = pl.BlockSpec(memory_space=pltpu.SMEM)
HBM = pl.BlockSpec(memory_space=pltpu.HBM)
CHEAP = pl.CostEstimate(flops=1000, bytes_accessed=1000, transcendentals=0)
PARAMS = pltpu.CompilerParams(vmem_limit_bytes=48 * 1024 * 1024)
LARGE = pltpu.CompilerParams(vmem_limit_bytes=57 * 1024 * 1024)
SMALL = pltpu.CompilerParams(vmem_limit_bytes=8 * 1024 * 1024)


def f32_of(*shape):
    return jax.ShapeDtypeStruct(shape, F32)


def split(a):
    top = a.astype(jnp.bfloat16)
    return top, (a - top.astype(F32)).astype(jnp.bfloat16)


def dot3(a, b, a_dim):
    dims = (((a_dim,), (0,)), ((), ()))
    a_top, a_low = split(a)
    b_top, b_low = split(b)
    one = functools.partial(lax.dot_general, dimension_numbers=dims, preferred_element_type=F32)
    return one(a_top, b_top) + (one(a_top, b_low) + one(a_low, b_top))


def take(refs, pieces):
    got = [refs[n][start : start + size, :] for n, start, size in pieces]
    return got[0] if len(got) == 1 else jnp.concatenate(got, 0)


def slab_copies(idx, slab, buf, sems):
    copies = []
    for i in range(buf.shape[0]):
        block = pl.ds(pl.multiple_of(idx[i] * 256, 256), 256)
        copies.append(pltpu.make_async_copy(slab.at[block, :], buf.at[i], sems.at[i]))
        copies[-1].start()
    return copies


def stage_kernel(plan, has_acc, idx, slab, *refs):
    refs, (out, buf, sems) = refs[:-3], refs[-3:]
    copies = slab_copies(idx, slab, buf, sems)
    for i, pieces in enumerate(plan):
        block = take(refs, pieces)
        copies[i].wait()
        term = dot3(buf[i], block, 0)
        if i == 0 and not has_acc:
            out[...] = term
        elif i == 0:
            out[...] = refs[-1][...] + term
        else:
            out[...] += term


def stage(slab_adj, blocks, plan, sources, acc=None):
    idx = jnp.stack([(jnp.asarray(cc & 7) * 2 + dd).astype(jnp.int32) for cc, dd in blocks])
    args = list(sources) + ([acc] if acc is not None else [])
    return pl.pallas_call(
        functools.partial(stage_kernel, plan, acc is not None),
        out_shape=f32_of(512, 256),
        in_specs=[SMEM, HBM] + [VMEM] * len(args),
        out_specs=VMEM,
        scratch_shapes=[pltpu.VMEM((len(plan), 256, 512), F32), pltpu.SemaphoreType.DMA((len(plan),))],
        compiler_params=PARAMS,
        cost_estimate=CHEAP,
    )(idx, slab_adj, *args)


def part_kernel(slab, cols, out):
    out[...] = dot3(slab[...], cols[...], 1)


def part_all(slab_adj, cols):
    return pl.pallas_call(
        part_kernel,
        out_shape=f32_of(4096, 256),
        grid=(8,),
        in_specs=[pl.BlockSpec((512, 512), lambda i: (i, 0)), pl.BlockSpec((512, 256), lambda i: (0, 0))],
        out_specs=pl.BlockSpec((512, 256), lambda i: (i, 0)),
        compiler_params=LARGE,
        cost_estimate=CHEAP,
    )(slab_adj, cols)


def last_kernel(idx, slab, block, acc, cols, ahead, keep, send, prod, diag, buf, sems):
    (copy,) = slab_copies(idx, slab, buf, sems)
    rest = acc[...]
    copy.wait()
    prod[...] = rest + dot3(buf[0], block[...], 0)
    cross = dot3(cols[...], prod[...], 0)
    diag[...] = ahead[...] - cross - cross.T
    for out, core in ((keep, idx[1]), (send, 1 - idx[1])):
        out[:256, :] = prod[pl.ds(pl.multiple_of(core * 256, 256), 256), :]
        out[256:, :] = diag[pl.ds(pl.multiple_of(core * 128, 128), 128), :]


def last(slab_adj, cc, dd, core, block, acc, cols, ahead):
    idx = jnp.stack([((cc & 7) * 2 + dd).astype(jnp.int32), core.astype(jnp.int32)])
    return pl.pallas_call(
        last_kernel,
        out_shape=(f32_of(384, 256), f32_of(384, 256)),
        in_specs=[SMEM, HBM] + [VMEM] * 4,
        out_specs=(VMEM, VMEM),
        scratch_shapes=[
            pltpu.VMEM((512, 256), F32),
            pltpu.VMEM((256, 256), F32),
            pltpu.VMEM((1, 256, 512), F32),
            pltpu.SemaphoreType.DMA((1,)),
        ],
        compiler_params=PARAMS,
        cost_estimate=CHEAP,
    )(idx, slab_adj, block, acc, cols, ahead)


def quarter_kernel(idx, kept, got, mine, *sends):
    for n, out in enumerate((mine,) + sends):
        y = (idx[0] + (0, 1, 3, 2)[n]) & 3
        for at, first, size in ((0, 0, 64), (64, 256, 32)):
            block = pl.ds(pl.multiple_of(first + y * size, size), size)
            out[at : at + size, :] = kept[block, :] + got[block, :]


def quarters(y, kept, got):
    return pl.pallas_call(
        quarter_kernel,
        out_shape=(f32_of(96, 256),) * 4,
        in_specs=[SMEM, VMEM, VMEM],
        out_specs=(VMEM,) * 4,
        compiler_params=SMALL,
        cost_estimate=CHEAP,
    )(y.astype(jnp.int32).reshape(1), kept, got)


def rows(a, start, size):
    return lax.dynamic_slice_in_dim(a, start, size, 0)


def z_shift(a, k):
    return lax.ppermute(a, "col", [(i, (i + k) % 8) for i in range(8)])


def z_xor(a, k):
    return lax.ppermute(a, "col", [(i, i ^ k) for i in range(8)])


def x_swap(a):
    return lax.ppermute(a, "depth", [(0, 1), (1, 0)])


def core_swap(a):
    return lax.ppermute(a, "row", [(i, i ^ 1) for i in range(16)])


def far_swap(a):
    return lax.ppermute(a, "row", [(i, i ^ 8) for i in range(16)])


def diagonal_swap(a):
    return lax.ppermute(a, ("row", "depth"), [(i, i ^ 17) for i in range(32)])


def y_shift(a, k):
    return lax.ppermute(a, "row", [(i, (i & 9) | ((((i >> 1) + k) & 3) << 1)) for i in range(16)])


def body(slab_adj, panel_rows, panel_cols, bar_rows, bar_cols, inv_diag, bar_diag):
    r = lax.axis_index("row")
    c = lax.axis_index("col")
    d = lax.axis_index("depth")
    core, y, far = r & 1, (r >> 1) & 3, r >> 3

    cat = lambda *a: jnp.concatenate(a, 0)
    hold = lax.optimization_barrier
    e = 1 - d

    own = panel_rows
    right, left, other = z_shift(own, 1), z_shift(own, -1), x_swap(own)
    product = stage(slab_adj, [(c, d)], [[(0, 0, 256)]], [own])
    part = part_all(slab_adj, panel_cols)

    def piece(cc):
        return rows(part, (cc & 7) * 512, 512)

    inv_t = inv_diag.T
    right, left, other, product, part, inv_t = hold((right, left, other, product, part, inv_t))

    next_x = x_swap(cat(right[:128], left[:128]))
    to_right, to_left = z_shift(cat(right, other[128:]), 1), z_shift(cat(other[128:], left), -1)
    product = stage(
        slab_adj,
        [(c, e), (c - 1, d), (c + 1, d)],
        [[(0, 0, 256)], [(1, 0, 256)], [(2, 0, 256)]],
        [other, right, left],
        product,
    )
    right, left, over_x, product = hold((to_right, to_left, next_x, product))

    def far_stage(k, right, left, over_x, product):
        return stage(
            slab_adj,
            [(c - k, d), (c + k, d), (c - k + 1, e), (c + k - 1, e)],
            [[(0, 0, 256)], [(1, 128, 256)], [(2, 0, 128), (0, 256, 128)], [(2, 128, 128), (1, 0, 128)]],
            [right, left, over_x],
            product,
        )

    next_x = x_swap(cat(right[:128], left[128:256]))
    to_right, to_left = z_shift(right, 1), z_shift(left, -1)
    product = far_stage(2, right, left, over_x, product)
    part_4 = piece(c + 4)
    right, left, over_x, product, part_4 = hold((to_right, to_left, next_x, product, part_4))

    next_x = x_swap(cat(right[:128], left[128:256]))
    to_right = z_shift(cat(right[128:], part_4[:256]), 1)
    to_left = z_shift(cat(left[:256], part_4[256:]), -1)
    product = far_stage(3, right, left, over_x, product)
    share = rows(bar_cols, r * 32, 32)
    share_cols = rows(panel_cols, r * 32, 32)
    ahead = dot_t(cat(bar_rows, share), cat(panel_rows, share_cols))
    right, left, over_x, product, ahead = hold((to_right, to_left, next_x, product, ahead))

    far_own = cat(left[128:256], right[:128])
    next_x = x_swap(far_own)
    part_r3, part_l3 = piece(c + 3), piece(c - 3)
    sum_r = z_shift(cat(part_r3[:256] + right[256:], part_r3[256:]), 1)
    sum_l = z_shift(cat(part_l3[:256], part_l3[256:] + left[256:]), -1)
    product = stage(
        slab_adj,
        [(c + 4, d), (c - 3, e), (c + 3, e)],
        [[(0, 0, 256)], [(3, 0, 128), (1, 128, 128)], [(3, 128, 128), (2, 0, 128)]],
        [far_own, right, left, over_x],
        product,
    )
    over_x, product = hold((next_x, product))

    keep, send = last(slab_adj, c + 4, e, core, over_x, product, panel_cols, ahead)
    v, sum_r, sum_l = hold((core_swap(send), sum_r, sum_l))
    sum_r, sum_l = z_shift(piece(c + 2) + sum_r, 1), z_shift(piece(c - 2) + sum_l, -1)
    mine, for_right, for_left, for_across = quarters(y, keep, v)
    v = mine + y_shift(for_right, 1) + y_shift(for_left, -1) + y_shift(for_across, 2)
    a, b, g = far_swap(v), x_swap(v[64:]), diagonal_swap(v[64:])
    a, b, g, sum_r, sum_l = hold((a, b, g, sum_r, sum_l))
    sum_r, sum_l = z_shift(piece(c + 1) + sum_r, 1), z_shift(piece(c - 1) + sum_l, -1)
    t = (v[64:] + b) + (a[64:] + g)
    t = t + z_xor(t, 1)
    t = (t + z_xor(t, 2)) + (z_xor(t, 4) + z_xor(t, 6))
    v = cat(v[:64] + a[:64], t)
    v, sum_r, sum_l = hold((v, sum_r, sum_l))
    whole = piece(c) + sum_r + sum_l
    over_x = x_swap(rows(whole, e * 256, 256))
    p1, m1, p2 = y_shift(v, -1), y_shift(v, 1), y_shift(v, 2)
    ring = cat(v, p1, p2, m1, v, p1, p2)
    ring = rows(ring, ((4 - y) & 3) * 96, 384).reshape(4, 96, 256)
    v = cat(ring[:, :64].reshape(256, 256), ring[:, 64:].reshape(128, 256))
    w = core_swap(v)
    first = core == 0
    lo, hi = jnp.where(first, v, w), jnp.where(first, w, v)
    term_cols = cat(lo[:256], hi[:256])
    total = cat(lo[256:], hi[256:])
    term_rows = rows(whole, d * 256, 256) + over_x
    adj_rows = dot(bar_rows - term_rows, inv_diag)
    adj_cols = dot(bar_cols - term_cols, inv_diag)
    diag_adj = bar_diag - dot(inv_t, total)
    return adj_rows, adj_cols, diag_adj


def solution(mesh):
    in_specs = (
        P("row", ("col", "depth")),
        P(("row", "col", "depth"), None),
        P(("col", "depth"), None),
        P(("row", "col", "depth"), None),
        P(("col", "depth"), None),
        P(),
        P(),
    )
    out_specs = (P(("row", "col", "depth"), None), P(("col", "depth"), None), P())
    return jax.shard_map(body, mesh=mesh, in_specs=in_specs, out_specs=out_specs, check_vma=False)
```

```python
import jax
import jax.numpy as jnp
from jax import lax
from jax.sharding import PartitionSpec as P

HIGH = lax.Precision.HIGH
F32 = jnp.float32


def dot(a, b):
    return jnp.dot(a, b, precision=HIGH, preferred_element_type=F32)


def dot_t(a, b):
    return lax.dot_general(a, b, (((0,), (0,)), ((), ())), precision=HIGH, preferred_element_type=F32)


def rows(a, start, size):
    return lax.dynamic_slice_in_dim(a, start, size, 0)


def z_shift(a, k):
    return lax.ppermute(a, "col", [(i, (i + k) % 8) for i in range(8)])


def z_xor(a, k):
    return lax.ppermute(a, "col", [(i, i ^ k) for i in range(8)])


def z_shift_other(a, k):
    return lax.ppermute(a, ("col", "depth"), [(i, ((i >> 1) + k) % 8 * 2 + (1 - (i & 1))) for i in range(16)])


def x_swap(a):
    return lax.ppermute(a, "depth", [(0, 1), (1, 0)])


def core_swap(a):
    return lax.ppermute(a, "row", [(i, i ^ 1) for i in range(16)])


def far_swap(a):
    return lax.ppermute(a, "row", [(i, i ^ 8) for i in range(16)])


def diagonal_swap(a):
    return lax.ppermute(a, ("row", "depth"), [(i, i ^ 17) for i in range(32)])


def y_shift(a, k):
    return lax.ppermute(a, "row", [(i, (i & 9) | ((((i >> 1) + k) & 3) << 1)) for i in range(16)])


def body(slab_adj, panel_rows, panel_cols, bar_rows, bar_cols, inv_diag, bar_diag):
    r = lax.axis_index("row")
    c = lax.axis_index("col")
    d = lax.axis_index("depth")
    core, y, far = r & 1, (r >> 1) & 3, r >> 3

    cat = lambda *a: jnp.concatenate(a, 0)
    hold = lax.optimization_barrier
    e = 1 - d

    def slab(cc, dd):
        return rows(slab_adj, ((cc & 7) * 2 + dd) * 256, 256)

    def add(product, blk, cc, dd):
        return product + dot_t(slab(cc, dd), blk)

    def part(cc, cols):
        return dot(rows(slab_adj, (cc & 7) * 512, 512), cols)

    own = panel_rows
    right, left, other = z_shift(own, 1), z_shift(own, -1), x_swap(own)
    part_4, part_r1 = part(c + 4, panel_cols), part(c + 1, panel_cols)
    inv_t = inv_diag.T
    right, left, other, part_4, part_r1, cols, inv_t, own = hold(
        (right, left, other, part_4, part_r1, panel_cols, inv_t, own)
    )

    over_x = x_swap(cat(right[:128], left[:128]))
    to_right, to_left = z_shift(cat(right, other[128:]), 1), z_shift(cat(other[128:], left), -1)
    product = dot_t(slab(c, d), own)
    product = add(product, other, c, e)
    first_right, first_left = right, left
    right, left, over_x, product, first_right, first_left, cols = hold(
        (to_right, to_left, over_x, product, first_right, first_left, cols)
    )

    def add_own(product, k, right, left):
        return add(add(product, right, c - k, d), left, c + k, d)

    def add_other(product, k, over_x, right_b, left_b):
        product = add(product, cat(over_x[:128], right_b), c - k, e)
        return add(product, cat(over_x[128:], left_b), c + k, e)

    next_x = x_swap(cat(right[:128], left[128:256]))
    to_right, to_left = z_shift(right, 1), z_shift(left, -1)
    product = add_own(product, 1, first_right, first_left)
    product = add_own(product, 2, right[:256], left[128:])
    product = add_other(product, 1, over_x, right[256:], left[:128])
    part_l1 = part(c - 1, cols)
    right, left, over_x, product, part_l1, part_4, cols = hold(
        (to_right, to_left, next_x, product, part_l1, part_4, cols)
    )

    next_x = x_swap(cat(right[:128], left[128:256]))
    to_right = z_shift(cat(right[128:], part_4[:256]), 1)
    to_left = z_shift(cat(left[:256], part_4[256:]), -1)
    from_right, from_left = z_shift_other(right[128:256], 1), z_shift_other(left[128:256], -1)
    product = add_own(product, 3, right[:256], left[128:])
    product = add_other(product, 2, over_x, right[256:], left[:128])
    part_r3, part_l3 = part(c + 3, cols), part(c - 3, cols)
    part_r2, part_l2 = part(c + 2, cols), part(c - 2, cols)
    share = rows(bar_cols, r * 32, 32)
    share_cols = rows(cols, r * 32, 32)
    ahead = dot_t(cat(bar_rows, share), cat(panel_rows, share_cols))
    right, left, over_x, from_right, from_left, product, part_r3, part_l3, part_r2, part_l2, ahead, cols = hold(
        (to_right, to_left, next_x, from_right, from_left, product, part_r3, part_l3, part_r2, part_l2, ahead, cols)
    )
    sum_r = z_shift(cat(part_r3[:256] + right[256:], part_r3[256:]), 1)
    sum_l = z_shift(cat(part_l3[:256], part_l3[256:] + left[256:]), -1)
    product = add(product, cat(left[128:256], right[:128]), c + 4, d)
    product = add(product, cat(from_left, from_right), c + 4, e)
    product = add_other(product, 3, over_x, right[128:256], left[:128])

    both = ahead - dot_t(cat(panel_cols, product), cat(product, panel_cols))

    def half(cc):
        return cat(rows(product, cc * 256, 256), rows(both, cc * 128, 128))

    v = half(core) + core_swap(half(1 - core))

    def quarter(yy):
        yy = yy & 3
        return cat(rows(v, yy * 64, 64), rows(v, 256 + yy * 32, 32))

    from_left, from_right, across = y_shift(quarter(y + 1), 1), y_shift(quarter(y - 1), -1), y_shift(quarter(y + 2), 2)
    from_left, sum_r, sum_l, cols = hold((from_left, sum_r, sum_l, cols))
    sum_r, sum_l = z_shift(part_r2 + sum_r, 1), z_shift(part_l2 + sum_l, -1)
    part_0 = part(c, cols)
    v = quarter(y) + from_left + from_right + across
    v, part_0 = hold((v, part_0))
    a, b, g = far_swap(v), x_swap(v[64:]), diagonal_swap(v[64:])
    t = (v[64:] + b) + (a[64:] + g)
    t = t + z_xor(t, 1)
    t, sum_r, sum_l = hold((t, sum_r, sum_l))
    sum_r, sum_l = z_shift(part_r1 + sum_r, 1), z_shift(part_l1 + sum_l, -1)
    t = t + z_xor(t, 2)
    t = t + z_xor(t, 6)
    v = cat(v[:64] + a[:64], t)
    p1, m1, p2 = y_shift(v, -1), y_shift(v, 1), y_shift(v, 2)
    p1, sum_r, sum_l = hold((p1, sum_r, sum_l))
    whole = part_0 + sum_r + sum_l
    over_x = x_swap(rows(whole, e * 256, 256))
    ring = cat(v, p1, p2, m1, v, p1, p2)
    ring = rows(ring, ((4 - y) & 3) * 96, 384).reshape(4, 96, 256)
    v = cat(ring[:, :64].reshape(256, 256), ring[:, 64:].reshape(128, 256))
    w = core_swap(v)
    first = core == 0
    lo, hi = jnp.where(first, v, w), jnp.where(first, w, v)
    term_cols = cat(lo[:256], hi[:256])
    total = cat(lo[256:], hi[256:])
    term_rows = rows(whole, d * 256, 256) + over_x
    adj_rows = dot(bar_rows - term_rows, inv_diag)
    adj_cols = dot(bar_cols - term_cols, inv_diag)
    diag_adj = bar_diag - dot(inv_t, total)
    return adj_rows, adj_cols, diag_adj


def solution(mesh):
    in_specs = (
        P("row", ("col", "depth")),
        P(("row", "col", "depth"), None),
        P(("col", "depth"), None),
        P(("row", "col", "depth"), None),
        P(("col", "depth"), None),
        P(),
        P(),
    )
    out_specs = (P(("row", "col", "depth"), None), P(("col", "depth"), None), P())
    return jax.shard_map(body, mesh=mesh, in_specs=in_specs, out_specs=out_specs, check_vma=False)
```

```python
import functools

import jax
import jax.numpy as jnp
from jax import lax
from jax.experimental import pallas as pl
from jax.experimental.pallas import tpu as pltpu
from jax.sharding import PartitionSpec as P

HIGH = lax.Precision.HIGH
F32 = jnp.float32


def dot(a, b):
    return jnp.dot(a, b, precision=HIGH, preferred_element_type=F32)


def dot_t(a, b):
    return lax.dot_general(a, b, (((0,), (0,)), ((), ())), precision=HIGH, preferred_element_type=F32)


def split(a):
    top = a.astype(jnp.bfloat16)
    return top, (a - top.astype(F32)).astype(jnp.bfloat16)


def dot3(a, b, a_dim):
    dims = (((a_dim,), (0,)), ((), ()))
    a_top, a_low = split(a)
    b_top, b_low = split(b)
    one = functools.partial(lax.dot_general, dimension_numbers=dims, preferred_element_type=F32)
    return one(a_top, b_top) + (one(a_top, b_low) + one(a_low, b_top))


def finish_kernel(idx, mine, got, bar_cols, bar_diag, inv, adj_cols, diag_adj, cols, total):
    for half, core in ((mine, idx[0]), (got, 1 - idx[0])):
        for j in range(4):
            y = (idx[1] + j) & 3
            cols[pl.ds(pl.multiple_of(core * 256 + y * 64, 64), 64), :] = half[j * 96 : j * 96 + 64, :]
            total[pl.ds(pl.multiple_of(core * 128 + y * 32, 32), 32), :] = half[j * 96 + 64 : j * 96 + 96, :]
    diag_adj[...] = bar_diag[...] - dot3(inv[...], total[...], 0)
    adj_cols[...] = dot3(bar_cols[...] - cols[...], inv[...], 1)


def finish(core, y, mine, got, bar_cols, bar_diag, inv):
    vmem = pl.BlockSpec(memory_space=pltpu.VMEM)
    return pl.pallas_call(
        finish_kernel,
        out_shape=(jax.ShapeDtypeStruct((512, 256), F32), jax.ShapeDtypeStruct((256, 256), F32)),
        in_specs=[pl.BlockSpec(memory_space=pltpu.SMEM)] + [vmem] * 5,
        out_specs=(vmem, vmem),
        scratch_shapes=[pltpu.VMEM((512, 256), F32), pltpu.VMEM((256, 256), F32)],
        compiler_params=pltpu.CompilerParams(vmem_limit_bytes=8 * 1024 * 1024),
        cost_estimate=pl.CostEstimate(flops=400_000_000, bytes_accessed=3_000_000, transcendentals=0),
    )(jnp.stack([core, y]).astype(jnp.int32), mine, got, bar_cols, bar_diag, inv)


def rows(a, start, size):
    return lax.dynamic_slice_in_dim(a, start, size, 0)


def z_shift(a, k):
    return lax.ppermute(a, "col", [(i, (i + k) % 8) for i in range(8)])


def z_xor(a, k):
    return lax.ppermute(a, "col", [(i, i ^ k) for i in range(8)])


def z_shift_other(a, k):
    return lax.ppermute(a, ("col", "depth"), [(i, ((i >> 1) + k) % 8 * 2 + (1 - (i & 1))) for i in range(16)])


def x_swap(a):
    return lax.ppermute(a, "depth", [(0, 1), (1, 0)])


def core_swap(a):
    return lax.ppermute(a, "row", [(i, i ^ 1) for i in range(16)])


def far_swap(a):
    return lax.ppermute(a, "row", [(i, i ^ 8) for i in range(16)])


def diagonal_swap(a):
    return lax.ppermute(a, ("row", "depth"), [(i, i ^ 17) for i in range(32)])


def y_shift(a, k):
    return lax.ppermute(a, "row", [(i, (i & 9) | ((((i >> 1) + k) & 3) << 1)) for i in range(16)])


def body(slab_adj, panel_rows, panel_cols, bar_rows, bar_cols, inv_diag, bar_diag):
    r = lax.axis_index("row")
    c = lax.axis_index("col")
    d = lax.axis_index("depth")
    core, y, far = r & 1, (r >> 1) & 3, r >> 3

    cat = lambda *a: jnp.concatenate(a, 0)
    hold = lax.optimization_barrier
    e = 1 - d

    def slab(cc, dd):
        return rows(slab_adj, ((cc & 7) * 2 + dd) * 256, 256)

    def add(product, blk, cc, dd):
        return product + dot_t(slab(cc, dd), blk)

    def part(cc, cols):
        return dot(rows(slab_adj, (cc & 7) * 512, 512), cols)

    own = panel_rows
    right, left, other = z_shift(own, 1), z_shift(own, -1), x_swap(own)
    part_4, part_r1 = part(c + 4, panel_cols), part(c + 1, panel_cols)
    sum_r, sum_l = z_shift(part_4[:256], 1), z_shift(part_4[256:], -1)
    right, left, other, part_r1, cols, own = hold((right, left, other, part_r1, panel_cols, own))

    over_x = x_swap(cat(right[:128], left[:128]))
    to_right, to_left = z_shift(cat(right, other[128:]), 1), z_shift(cat(other[128:], left), -1)
    product = dot_t(slab(c, d), own)
    product = add(product, other, c, e)
    first_right, first_left = right, left
    right, left, over_x, product, first_right, first_left, sum_r, sum_l, cols = hold(
        (to_right, to_left, over_x, product, first_right, first_left, sum_r, sum_l, cols)
    )

    def add_own(product, k, right, left):
        return add(add(product, right, c - k, d), left, c + k, d)

    def add_other(product, k, over_x, right_b, left_b):
        product = add(product, cat(over_x[:128], right_b), c - k, e)
        return add(product, cat(over_x[128:], left_b), c + k, e)

    next_x = x_swap(cat(right[:128], left[128:256]))
    to_right, to_left = z_shift(right, 1), z_shift(left, -1)
    product = add_own(product, 1, first_right, first_left)
    product = add_own(product, 2, right[:256], left[128:])
    product = add_other(product, 1, over_x, right[256:], left[:128])
    part_l1 = part(c - 1, cols)
    right, left, over_x, product, part_l1, cols = hold((to_right, to_left, next_x, product, part_l1, cols))

    next_x = x_swap(cat(right[:128], left[128:256]))
    to_right, to_left = z_shift(right[128:], 1), z_shift(left[:256], -1)
    from_right, from_left = z_shift_other(right[128:256], 1), z_shift_other(left[128:256], -1)
    product = add_own(product, 3, right[:256], left[128:])
    product = add_other(product, 2, over_x, right[256:], left[:128])
    part_r3, part_l3 = part(c + 3, cols), part(c - 3, cols)
    part_r2, part_l2 = part(c + 2, cols), part(c - 2, cols)
    share = rows(bar_cols, r * 32, 32)
    share_cols = rows(cols, r * 32, 32)
    ahead = dot_t(cat(bar_rows, share), cat(panel_rows, share_cols))
    right, left, over_x, from_right, from_left, product, part_r3, part_l3, part_r2, part_l2, ahead, cols = hold(
        (to_right, to_left, next_x, from_right, from_left, product, part_r3, part_l3, part_r2, part_l2, ahead, cols)
    )
    sum_r = z_shift(cat(part_r3[:256] + sum_r, part_r3[256:]), 1)
    sum_l = z_shift(cat(part_l3[:256], part_l3[256:] + sum_l), -1)
    product = add(product, cat(left[128:256], right[:128]), c + 4, d)
    product = add(product, cat(from_left, from_right), c + 4, e)
    product = add_other(product, 3, over_x, right[128:256], left[:128])

    both = ahead - dot_t(cat(panel_cols, product), cat(product, panel_cols))

    def half(cc):
        return cat(rows(product, cc * 256, 256), rows(both, cc * 128, 128))

    v = half(core) + core_swap(half(1 - core))

    def quarter(yy):
        yy = yy & 3
        return cat(rows(v, yy * 64, 64), rows(v, 256 + yy * 32, 32))

    from_left, from_right, across = y_shift(quarter(y + 1), 1), y_shift(quarter(y - 1), -1), y_shift(quarter(y + 2), 2)
    from_left, sum_r, sum_l, cols = hold((from_left, sum_r, sum_l, cols))
    sum_r, sum_l = z_shift(part_r2 + sum_r, 1), z_shift(part_l2 + sum_l, -1)
    part_0 = part(c, cols)
    v = quarter(y) + from_left + from_right + across
    v, part_0 = hold((v, part_0))
    a, b, g = far_swap(v), x_swap(v[64:]), diagonal_swap(v[64:])
    t = (v[64:] + b) + (a[64:] + g)
    t = t + z_xor(t, 1)
    t, sum_r, sum_l = hold((t, sum_r, sum_l))
    t = t + z_xor(t, 2)
    t, sum_r, sum_l = hold((t, sum_r, sum_l))
    sum_r, sum_l = z_shift(part_r1 + sum_r, 1), z_shift(part_l1 + sum_l, -1)
    t = t + z_xor(t, 6)
    v = cat(v[:64] + a[:64], t)
    p1, m1, p2 = y_shift(v, -1), y_shift(v, 1), y_shift(v, 2)
    p1, sum_r, sum_l = hold((p1, sum_r, sum_l))
    whole = part_0 + sum_r + sum_l
    over_x = x_swap(rows(whole, e * 256, 256))
    v = cat(v, p1, p2, m1)
    adj_cols, diag_adj = finish(core, y, v, core_swap(v), bar_cols, bar_diag, inv_diag)
    term_rows = rows(whole, d * 256, 256) + over_x
    adj_rows = dot(bar_rows - term_rows, inv_diag)
    return adj_rows, adj_cols, diag_adj


def solution(mesh):
    in_specs = (
        P("row", ("col", "depth")),
        P(("row", "col", "depth"), None),
        P(("col", "depth"), None),
        P(("row", "col", "depth"), None),
        P(("col", "depth"), None),
        P(),
        P(),
    )
    out_specs = (P(("row", "col", "depth"), None), P(("col", "depth"), None), P())
    return jax.shard_map(body, mesh=mesh, in_specs=in_specs, out_specs=out_specs, check_vma=False)
```

```python
import functools

import jax
import jax.numpy as jnp
from jax import lax
from jax.experimental import pallas as pl
from jax.experimental.pallas import tpu as pltpu
from jax.sharding import PartitionSpec as P

HIGH = lax.Precision.HIGH
F32 = jnp.float32


def dot(a, b):
    return jnp.dot(a, b, precision=HIGH, preferred_element_type=F32)


def dot_t(a, b):
    return lax.dot_general(a, b, (((0,), (0,)), ((), ())), precision=HIGH, preferred_element_type=F32)


def split(a):
    top = a.astype(jnp.bfloat16)
    return top, (a - top.astype(F32)).astype(jnp.bfloat16)


def dot3(a, b, a_dim):
    dims = (((a_dim,), (0,)), ((), ()))
    a_top, a_low = split(a)
    b_top, b_low = split(b)
    one = functools.partial(lax.dot_general, dimension_numbers=dims, preferred_element_type=F32)
    return one(a_top, b_top) + (one(a_top, b_low) + one(a_low, b_top))


def finish_kernel(idx, mine, got, bar_cols, bar_diag, inv, adj_cols, diag_adj, cols, total):
    for half, core in ((mine, idx[0]), (got, 1 - idx[0])):
        for j in range(4):
            y = (idx[1] + j) & 3
            cols[pl.ds(pl.multiple_of(core * 256 + y * 64, 64), 64), :] = half[j * 96 : j * 96 + 64, :]
            total[pl.ds(pl.multiple_of(core * 128 + y * 32, 32), 32), :] = half[j * 96 + 64 : j * 96 + 96, :]
    diag_adj[...] = bar_diag[...] - dot3(inv[...], total[...], 0)
    adj_cols[...] = dot3(bar_cols[...] - cols[...], inv[...], 1)


def finish(core, y, mine, got, bar_cols, bar_diag, inv):
    vmem = pl.BlockSpec(memory_space=pltpu.VMEM)
    return pl.pallas_call(
        finish_kernel,
        out_shape=(jax.ShapeDtypeStruct((512, 256), F32), jax.ShapeDtypeStruct((256, 256), F32)),
        in_specs=[pl.BlockSpec(memory_space=pltpu.SMEM)] + [vmem] * 5,
        out_specs=(vmem, vmem),
        scratch_shapes=[pltpu.VMEM((512, 256), F32), pltpu.VMEM((256, 256), F32)],
        compiler_params=pltpu.CompilerParams(vmem_limit_bytes=8 * 1024 * 1024),
        cost_estimate=pl.CostEstimate(flops=400_000_000, bytes_accessed=3_000_000, transcendentals=0),
    )(jnp.stack([core, y]).astype(jnp.int32), mine, got, bar_cols, bar_diag, inv)


def rows(a, start, size):
    return lax.dynamic_slice_in_dim(a, start, size, 0)


def z_shift(a, k):
    return lax.ppermute(a, "col", [(i, (i + k) % 8) for i in range(8)])


def z_xor(a, k):
    return lax.ppermute(a, "col", [(i, i ^ k) for i in range(8)])


def z_shift_other(a, k):
    return lax.ppermute(a, ("col", "depth"), [(i, ((i >> 1) + k) % 8 * 2 + (1 - (i & 1))) for i in range(16)])


def x_swap(a):
    return lax.ppermute(a, "depth", [(0, 1), (1, 0)])


def core_swap(a):
    return lax.ppermute(a, "row", [(i, i ^ 1) for i in range(16)])


def far_swap(a):
    return lax.ppermute(a, "row", [(i, i ^ 8) for i in range(16)])


def diagonal_swap(a):
    return lax.ppermute(a, ("row", "depth"), [(i, i ^ 17) for i in range(32)])


def y_shift(a, k):
    return lax.ppermute(a, "row", [(i, (i & 9) | ((((i >> 1) + k) & 3) << 1)) for i in range(16)])


def body(slab_adj, panel_rows, panel_cols, bar_rows, bar_cols, inv_diag, bar_diag):
    r = lax.axis_index("row")
    c = lax.axis_index("col")
    d = lax.axis_index("depth")
    core, y, far = r & 1, (r >> 1) & 3, r >> 3

    cat = lambda *a: jnp.concatenate(a, 0)
    hold = lax.optimization_barrier
    e = 1 - d

    def slab(cc, dd):
        return rows(slab_adj, ((cc & 7) * 2 + dd) * 256, 256)

    def add(product, blk, cc, dd):
        return product + dot_t(slab(cc, dd), blk)

    def part(cc, cols):
        return dot(rows(slab_adj, (cc & 7) * 512, 512), cols)

    own = panel_rows
    right, left, other = z_shift(own, 1), z_shift(own, -1), x_swap(own)
    part_4 = part(c + 4, panel_cols)
    sum_r, sum_l = z_shift(part_4[:256], 1), z_shift(part_4[256:], -1)
    right, left, other, cols, own = hold((right, left, other, panel_cols, own))

    over_x = x_swap(cat(right[:128], left[:128]))
    to_right, to_left = z_shift(cat(right, other[128:]), 1), z_shift(cat(other[128:], left), -1)
    part_r3, part_l3 = part(c + 3, cols), part(c - 3, cols)
    share = rows(bar_cols, r * 32, 32)
    share_cols = rows(cols, r * 32, 32)
    ahead = dot_t(cat(bar_rows, share), cat(panel_rows, share_cols))
    first_right, first_left = right, left
    right, left, over_x, ahead, first_right, first_left, sum_r, sum_l, part_r3, part_l3, cols, own, other = hold(
        (to_right, to_left, over_x, ahead, first_right, first_left, sum_r, sum_l, part_r3, part_l3, cols, own, other)
    )

    def add_own(product, k, right, left):
        return add(add(product, right, c - k, d), left, c + k, d)

    def add_other(product, k, over_x, right_b, left_b):
        product = add(product, cat(over_x[:128], right_b), c - k, e)
        return add(product, cat(over_x[128:], left_b), c + k, e)

    next_x = x_swap(cat(right[:128], left[128:256]))
    to_right, to_left = z_shift(right, 1), z_shift(left, -1)
    product = add(dot_t(slab(c, d), own), other, c, e)
    product = add_own(product, 1, first_right, first_left)
    product = add_own(product, 2, right[:256], left[128:])
    product = add_other(product, 1, over_x, right[256:], left[:128])
    sum_r = z_shift(cat(part_r3[:256] + sum_r, part_r3[256:]), 1)
    sum_l = z_shift(cat(part_l3[:256], part_l3[256:] + sum_l), -1)
    right, left, over_x, product, cols = hold((to_right, to_left, next_x, product, cols))

    next_x = x_swap(cat(right[:128], left[128:256]))
    to_right, to_left = z_shift(right[128:], 1), z_shift(left[:256], -1)
    from_right, from_left = z_shift_other(right[128:256], 1), z_shift_other(left[128:256], -1)
    product = add_own(product, 3, right[:256], left[128:])
    product = add_other(product, 2, over_x, right[256:], left[:128])
    sum_r, sum_l, cols = hold((sum_r, sum_l, cols))
    part_r2, part_l2 = part(c + 2, cols), part(c - 2, cols)
    right, left, over_x, from_right, from_left, product, part_r2, part_l2, cols, sum_r, sum_l = hold(
        (
            to_right, to_left, next_x, from_right, from_left, product,
            part_r2, part_l2, cols, sum_r, sum_l,
        )
    )
    sum_r, sum_l = z_shift(part_r2 + sum_r, 1), z_shift(part_l2 + sum_l, -1)
    product = add(product, cat(left[128:256], right[:128]), c + 4, d)
    product = add(product, cat(from_left, from_right), c + 4, e)
    product = add_other(product, 3, over_x, right[128:256], left[:128])

    both = ahead - dot_t(cat(panel_cols, product), cat(product, panel_cols))

    def half(cc):
        return cat(rows(product, cc * 256, 256), rows(both, cc * 128, 128))

    v = half(core) + core_swap(half(1 - core))

    def quarter(yy):
        yy = yy & 3
        return cat(rows(v, yy * 64, 64), rows(v, 256 + yy * 32, 32))

    from_left, from_right, across = y_shift(quarter(y + 1), 1), y_shift(quarter(y - 1), -1), y_shift(quarter(y + 2), 2)
    part_r1, part_l1 = part(c + 1, cols), part(c - 1, cols)
    from_left, sum_r, sum_l, part_r1, part_l1, cols = hold((from_left, sum_r, sum_l, part_r1, part_l1, cols))
    sum_r, sum_l = z_shift(part_r1 + sum_r, 1), z_shift(part_l1 + sum_l, -1)
    part_0 = part(c, cols)
    v = quarter(y) + from_left + from_right + across
    v, part_0 = hold((v, part_0))
    a, b, g = far_swap(v), x_swap(v[64:]), diagonal_swap(v[64:])
    t = (v[64:] + b) + (a[64:] + g)
    t = t + z_xor(t, 1)
    t, sum_r, sum_l, part_0 = hold((t, sum_r, sum_l, part_0))
    whole = part_0 + sum_r + sum_l
    over_x = x_swap(rows(whole, e * 256, 256))
    t = t + z_xor(t, 2)
    t = t + z_xor(t, 6)
    v = cat(v[:64] + a[:64], t)
    p1, m1, p2 = y_shift(v, -1), y_shift(v, 1), y_shift(v, 2)
    v = cat(v, p1, p2, m1)
    adj_cols, diag_adj = finish(core, y, v, core_swap(v), bar_cols, bar_diag, inv_diag)
    term_rows = rows(whole, d * 256, 256) + over_x
    adj_rows = dot(bar_rows - term_rows, inv_diag)
    return adj_rows, adj_cols, diag_adj


def solution(mesh):
    in_specs = (
        P("row", ("col", "depth")),
        P(("row", "col", "depth"), None),
        P(("col", "depth"), None),
        P(("row", "col", "depth"), None),
        P(("col", "depth"), None),
        P(),
        P(),
    )
    out_specs = (P(("row", "col", "depth"), None), P(("col", "depth"), None), P())
    return jax.shard_map(body, mesh=mesh, in_specs=in_specs, out_specs=out_specs, check_vma=False)
```

```python
import functools

import jax
import jax.numpy as jnp
from jax import lax
from jax.experimental import pallas as pl
from jax.experimental.pallas import tpu as pltpu
from jax.sharding import PartitionSpec as P

HIGH = lax.Precision.HIGH
F32 = jnp.float32


def dot(a, b):
    return jnp.dot(a, b, precision=HIGH, preferred_element_type=F32)


def dot_t(a, b):
    return lax.dot_general(a, b, (((0,), (0,)), ((), ())), precision=HIGH, preferred_element_type=F32)


def split(a):
    top = a.astype(jnp.bfloat16)
    return top, (a - top.astype(F32)).astype(jnp.bfloat16)


def dot3(a, b, a_dim):
    dims = (((a_dim,), (0,)), ((), ()))
    a_top, a_low = split(a)
    b_top, b_low = split(b)
    one = functools.partial(lax.dot_general, dimension_numbers=dims, preferred_element_type=F32)
    return one(a_top, b_top) + (one(a_top, b_low) + one(a_low, b_top))


def finish_kernel(idx, mine, got, bar_cols, bar_diag, inv, adj_cols, diag_adj, cols, total):
    for half, core in ((mine, idx[0]), (got, 1 - idx[0])):
        for j in range(4):
            y = (idx[1] + j) & 3
            cols[pl.ds(pl.multiple_of(core * 256 + y * 64, 64), 64), :] = half[j * 96 : j * 96 + 64, :]
            total[pl.ds(pl.multiple_of(core * 128 + y * 32, 32), 32), :] = half[j * 96 + 64 : j * 96 + 96, :]
    diag_adj[...] = bar_diag[...] - dot3(inv[...], total[...], 0)
    adj_cols[...] = dot3(bar_cols[...] - cols[...], inv[...], 1)


def finish(core, y, mine, got, bar_cols, bar_diag, inv):
    vmem = pl.BlockSpec(memory_space=pltpu.VMEM)
    return pl.pallas_call(
        finish_kernel,
        out_shape=(jax.ShapeDtypeStruct((512, 256), F32), jax.ShapeDtypeStruct((256, 256), F32)),
        in_specs=[pl.BlockSpec(memory_space=pltpu.SMEM)] + [vmem] * 5,
        out_specs=(vmem, vmem),
        scratch_shapes=[pltpu.VMEM((512, 256), F32), pltpu.VMEM((256, 256), F32)],
        compiler_params=pltpu.CompilerParams(vmem_limit_bytes=8 * 1024 * 1024),
        cost_estimate=pl.CostEstimate(flops=400_000_000, bytes_accessed=3_000_000, transcendentals=0),
    )(jnp.stack([core, y]).astype(jnp.int32), mine, got, bar_cols, bar_diag, inv)


def rows(a, start, size):
    return lax.dynamic_slice_in_dim(a, start, size, 0)


def z_shift(a, k):
    return lax.ppermute(a, "col", [(i, (i + k) % 8) for i in range(8)])


def z_xor(a, k):
    return lax.ppermute(a, "col", [(i, i ^ k) for i in range(8)])


def z_shift_other(a, k):
    return lax.ppermute(a, ("col", "depth"), [(i, ((i >> 1) + k) % 8 * 2 + (1 - (i & 1))) for i in range(16)])


def x_swap(a):
    return lax.ppermute(a, "depth", [(0, 1), (1, 0)])


def core_swap(a):
    return lax.ppermute(a, "row", [(i, i ^ 1) for i in range(16)])


def far_swap(a):
    return lax.ppermute(a, "row", [(i, i ^ 8) for i in range(16)])


def diagonal_swap(a):
    return lax.ppermute(a, ("row", "depth"), [(i, i ^ 17) for i in range(32)])


def y_shift(a, k):
    return lax.ppermute(a, "row", [(i, (i & 9) | ((((i >> 1) + k) & 3) << 1)) for i in range(16)])


def body(slab_adj, panel_rows, panel_cols, bar_rows, bar_cols, inv_diag, bar_diag):
    r = lax.axis_index("row")
    c = lax.axis_index("col")
    d = lax.axis_index("depth")
    core, y, far = r & 1, (r >> 1) & 3, r >> 3

    cat = lambda *a: jnp.concatenate(a, 0)
    hold = lax.optimization_barrier
    e = 1 - d

    def slab(cc, dd):
        return rows(slab_adj, ((cc & 7) * 2 + dd) * 256, 256)

    def add(product, blk, cc, dd):
        return product + dot_t(slab(cc, dd), blk)

    def part(cc, cols):
        return dot(rows(slab_adj, (cc & 7) * 512, 512), cols)

    own = panel_rows
    right, left, other = z_shift(own, 1), z_shift(own, -1), x_swap(own)
    part_4, part_0 = part(c + 4, panel_cols), part(c, panel_cols)
    sum_r, sum_l = z_shift(part_4[:256], 1), z_shift(part_4[256:], -1)
    right, left, other, part_0, cols, own = hold((right, left, other, part_0, panel_cols, own))

    over_x = x_swap(cat(right[:128], left[:128]))
    to_right, to_left = z_shift(cat(right, other[128:]), 1), z_shift(cat(other[128:], left), -1)
    share = rows(bar_cols, r * 32, 32)
    share_cols = rows(cols, r * 32, 32)
    ahead = dot_t(cat(bar_rows, share), cat(panel_rows, share_cols))
    first_right, first_left = right, left
    right, left, over_x, ahead, first_right, first_left, sum_r, sum_l, cols, own, other = hold(
        (to_right, to_left, over_x, ahead, first_right, first_left, sum_r, sum_l, cols, own, other)
    )

    def add_own(product, k, right, left):
        return add(add(product, right, c - k, d), left, c + k, d)

    def add_other(product, k, over_x, right_b, left_b):
        product = add(product, cat(over_x[:128], right_b), c - k, e)
        return add(product, cat(over_x[128:], left_b), c + k, e)

    next_x = x_swap(cat(right[:128], left[128:256]))
    to_right, to_left = z_shift(right, 1), z_shift(left, -1)
    product = add(dot_t(slab(c, d), own), other, c, e)
    product = add_own(product, 1, first_right, first_left)
    product = add_own(product, 2, right[:256], left[128:])
    product = add_other(product, 1, over_x, right[256:], left[:128])
    sum_0 = x_swap(rows(part_0, e * 256, 256))
    right, left, over_x, product, sum_0, cols = hold((to_right, to_left, next_x, product, sum_0, cols))

    next_x = x_swap(cat(right[:128], left[128:256]))
    to_right, to_left = z_shift(right[128:], 1), z_shift(left[:256], -1)
    from_right, from_left = z_shift_other(right[128:256], 1), z_shift_other(left[128:256], -1)
    product = add_own(product, 3, right[:256], left[128:])
    product = add_other(product, 2, over_x, right[256:], left[:128])
    part_r3, part_l3 = part(c + 3, cols), part(c - 3, cols)
    right, left, over_x, from_right, from_left, product, part_r3, part_l3, ahead, cols = hold(
        (to_right, to_left, next_x, from_right, from_left, product, part_r3, part_l3, ahead, cols)
    )
    sum_r = z_shift(cat(part_r3[:256] + sum_r, part_r3[256:]), 1)
    sum_l = z_shift(cat(part_l3[:256], part_l3[256:] + sum_l), -1)
    product = add(product, cat(left[128:256], right[:128]), c + 4, d)
    product = add(product, cat(from_left, from_right), c + 4, e)
    product = add_other(product, 3, over_x, right[128:256], left[:128])

    both = ahead - dot_t(cat(panel_cols, product), cat(product, panel_cols))

    def half(cc):
        return cat(rows(product, cc * 256, 256), rows(both, cc * 128, 128))

    v = half(core) + core_swap(half(1 - core))

    def quarter(yy):
        yy = yy & 3
        return cat(rows(v, yy * 64, 64), rows(v, 256 + yy * 32, 32))

    from_left, from_right, across = y_shift(quarter(y + 1), 1), y_shift(quarter(y - 1), -1), y_shift(quarter(y + 2), 2)
    part_r2, part_l2 = part(c + 2, cols), part(c - 2, cols)
    from_left, sum_r, sum_l, part_r2, part_l2, cols = hold((from_left, sum_r, sum_l, part_r2, part_l2, cols))
    sum_r, sum_l = z_shift(part_r2 + sum_r, 1), z_shift(part_l2 + sum_l, -1)
    part_r1, part_l1 = part(c + 1, cols), part(c - 1, cols)
    v = quarter(y) + from_left + from_right + across
    v, part_r1 = hold((v, part_r1))
    a, b, g = far_swap(v), x_swap(v[64:]), diagonal_swap(v[64:])
    t = (v[64:] + b) + (a[64:] + g)
    t = t + z_xor(t, 1)
    t, sum_r, sum_l, part_r1, part_l1 = hold((t, sum_r, sum_l, part_r1, part_l1))
    sum_r, sum_l = part_r1 + sum_r, part_l1 + sum_l
    got = x_swap(cat(rows(sum_r, e * 256, 256), rows(sum_l, e * 256, 256)))
    t = t + z_xor(t, 2)
    t = t + z_xor(t, 6)
    v = cat(v[:64] + a[:64], t)
    p1, m1, p2 = y_shift(v, -1), y_shift(v, 1), y_shift(v, 2)
    p1, got = hold((p1, got))
    sum_r = z_shift(rows(sum_r, d * 256, 256) + got[:256], 1)
    sum_l = z_shift(rows(sum_l, d * 256, 256) + got[256:], -1)
    v = cat(v, p1, p2, m1)
    adj_cols, diag_adj = finish(core, y, v, core_swap(v), bar_cols, bar_diag, inv_diag)
    term_rows = rows(part_0, d * 256, 256) + sum_0 + sum_r + sum_l
    adj_rows = dot(bar_rows - term_rows, inv_diag)
    return adj_rows, adj_cols, diag_adj


def solution(mesh):
    in_specs = (
        P("row", ("col", "depth")),
        P(("row", "col", "depth"), None),
        P(("col", "depth"), None),
        P(("row", "col", "depth"), None),
        P(("col", "depth"), None),
        P(),
        P(),
    )
    out_specs = (P(("row", "col", "depth"), None), P(("col", "depth"), None), P())
    return jax.shard_map(body, mesh=mesh, in_specs=in_specs, out_specs=out_specs, check_vma=False)
```

```python
import functools

import jax
import jax.numpy as jnp
from jax import lax
from jax.experimental import pallas as pl
from jax.experimental.pallas import tpu as pltpu
from jax.sharding import PartitionSpec as P

HIGH = lax.Precision.HIGH
F32 = jnp.float32


def dot(a, b):
    return jnp.dot(a, b, precision=HIGH, preferred_element_type=F32)


def dot_t(a, b):
    return lax.dot_general(a, b, (((0,), (0,)), ((), ())), precision=HIGH, preferred_element_type=F32)


def split(a):
    top = a.astype(jnp.bfloat16)
    return top, (a - top.astype(F32)).astype(jnp.bfloat16)


def dot3(a, b, a_dim):
    dims = (((a_dim,), (0,)), ((), ()))
    a_top, a_low = split(a)
    b_top, b_low = split(b)
    one = functools.partial(lax.dot_general, dimension_numbers=dims, preferred_element_type=F32)
    return one(a_top, b_top) + (one(a_top, b_low) + one(a_low, b_top))


def finish_kernel(
    idx, mine, got, bar_cols, bar_diag, inv, rest, sum_r, sum_l, adj_rows, adj_cols, diag_adj, cols, total
):
    adj_rows[...] = dot3(rest[...] - sum_r[...] - sum_l[...], inv[...], 1)
    for half, core in ((mine, idx[0]), (got, 1 - idx[0])):
        for j in range(4):
            y = (idx[1] + j) & 3
            cols[pl.ds(pl.multiple_of(core * 256 + y * 64, 64), 64), :] = half[j * 96 : j * 96 + 64, :]
            total[pl.ds(pl.multiple_of(core * 128 + y * 32, 32), 32), :] = half[j * 96 + 64 : j * 96 + 96, :]
    diag_adj[...] = bar_diag[...] - dot3(inv[...], total[...], 0)
    adj_cols[...] = dot3(bar_cols[...] - cols[...], inv[...], 1)


def finish(core, y, mine, got, bar_cols, bar_diag, inv, rest, sum_r, sum_l):
    vmem = pl.BlockSpec(memory_space=pltpu.VMEM)
    return pl.pallas_call(
        finish_kernel,
        out_shape=tuple(jax.ShapeDtypeStruct((n, 256), F32) for n in (256, 512, 256)),
        in_specs=[pl.BlockSpec(memory_space=pltpu.SMEM)] + [vmem] * 8,
        out_specs=(vmem, vmem, vmem),
        scratch_shapes=[pltpu.VMEM((512, 256), F32), pltpu.VMEM((256, 256), F32)],
        compiler_params=pltpu.CompilerParams(vmem_limit_bytes=8 * 1024 * 1024),
        cost_estimate=pl.CostEstimate(flops=400_000_000, bytes_accessed=3_000_000, transcendentals=0),
    )(jnp.stack([core, y]).astype(jnp.int32), mine, got, bar_cols, bar_diag, inv, rest, sum_r, sum_l)


def rows(a, start, size):
    return lax.dynamic_slice_in_dim(a, start, size, 0)


def z_shift(a, k):
    return lax.ppermute(a, "col", [(i, (i + k) % 8) for i in range(8)])


def z_xor(a, k):
    return lax.ppermute(a, "col", [(i, i ^ k) for i in range(8)])


def z_shift_other(a, k):
    return lax.ppermute(a, ("col", "depth"), [(i, ((i >> 1) + k) % 8 * 2 + (1 - (i & 1))) for i in range(16)])


def x_swap(a):
    return lax.ppermute(a, "depth", [(0, 1), (1, 0)])


def core_swap(a):
    return lax.ppermute(a, "row", [(i, i ^ 1) for i in range(16)])


def far_swap(a):
    return lax.ppermute(a, "row", [(i, i ^ 8) for i in range(16)])


def diagonal_swap(a):
    return lax.ppermute(a, ("row", "depth"), [(i, i ^ 17) for i in range(32)])


def y_shift(a, k):
    return lax.ppermute(a, "row", [(i, (i & 9) | ((((i >> 1) + k) & 3) << 1)) for i in range(16)])


def body(slab_adj, panel_rows, panel_cols, bar_rows, bar_cols, inv_diag, bar_diag):
    r = lax.axis_index("row")
    c = lax.axis_index("col")
    d = lax.axis_index("depth")
    core, y, far = r & 1, (r >> 1) & 3, r >> 3

    cat = lambda *a: jnp.concatenate(a, 0)
    hold = lax.optimization_barrier
    e = 1 - d

    def slab(cc, dd):
        return rows(slab_adj, ((cc & 7) * 2 + dd) * 256, 256)

    def add(product, blk, cc, dd):
        return product + dot_t(slab(cc, dd), blk)

    def part(cc, cols):
        return dot(rows(slab_adj, (cc & 7) * 512, 512), cols)

    own = panel_rows
    right, left, other = z_shift(own, 1), z_shift(own, -1), x_swap(own)
    part_4, part_0 = part(c + 4, panel_cols), part(c, panel_cols)
    sum_r, sum_l = z_shift(part_4[:256], 1), z_shift(part_4[256:], -1)
    right, left, other, part_0, cols, own = hold((right, left, other, part_0, panel_cols, own))

    over_x = x_swap(cat(right[:128], left[:128]))
    to_right, to_left = z_shift(cat(right, other[128:]), 1), z_shift(cat(other[128:], left), -1)
    share = rows(bar_cols, r * 32, 32)
    share_cols = rows(cols, r * 32, 32)
    ahead = dot_t(cat(bar_rows, share), cat(panel_rows, share_cols))
    first_right, first_left = right, left
    right, left, over_x, ahead, first_right, first_left, sum_r, sum_l, cols, own, other = hold(
        (to_right, to_left, over_x, ahead, first_right, first_left, sum_r, sum_l, cols, own, other)
    )

    def add_own(product, k, right, left):
        return add(add(product, right, c - k, d), left, c + k, d)

    def add_other(product, k, over_x, right_b, left_b):
        product = add(product, cat(over_x[:128], right_b), c - k, e)
        return add(product, cat(over_x[128:], left_b), c + k, e)

    next_x = x_swap(cat(right[:128], left[128:256]))
    to_right, to_left = z_shift(right, 1), z_shift(left, -1)
    product = add(dot_t(slab(c, d), own), other, c, e)
    product = add_own(product, 1, first_right, first_left)
    product = add_own(product, 2, right[:256], left[128:])
    product = add_other(product, 1, over_x, right[256:], left[:128])
    sum_0 = x_swap(rows(part_0, e * 256, 256))
    right, left, over_x, product, sum_0, cols = hold((to_right, to_left, next_x, product, sum_0, cols))

    next_x = x_swap(cat(right[:128], left[128:256]))
    to_right, to_left = z_shift(right[128:], 1), z_shift(left[:256], -1)
    from_right, from_left = z_shift_other(right[128:256], 1), z_shift_other(left[128:256], -1)
    product = add_own(product, 3, right[:256], left[128:])
    product = add_other(product, 2, over_x, right[256:], left[:128])
    part_r3, part_l3 = part(c + 3, cols), part(c - 3, cols)
    right, left, over_x, from_right, from_left, product, part_r3, part_l3, ahead, cols = hold(
        (to_right, to_left, next_x, from_right, from_left, product, part_r3, part_l3, ahead, cols)
    )
    sum_r = z_shift(cat(part_r3[:256] + sum_r, part_r3[256:]), 1)
    sum_l = z_shift(cat(part_l3[:256], part_l3[256:] + sum_l), -1)
    product = add(product, cat(left[128:256], right[:128]), c + 4, d)
    product = add(product, cat(from_left, from_right), c + 4, e)
    product = add_other(product, 3, over_x, right[128:256], left[:128])

    both = ahead - dot_t(cat(panel_cols, product), cat(product, panel_cols))

    def half(cc):
        return cat(rows(product, cc * 256, 256), rows(both, cc * 128, 128))

    v = half(core) + core_swap(half(1 - core))

    def quarter(yy):
        yy = yy & 3
        return cat(rows(v, yy * 64, 64), rows(v, 256 + yy * 32, 32))

    from_left, from_right, across = y_shift(quarter(y + 1), 1), y_shift(quarter(y - 1), -1), y_shift(quarter(y + 2), 2)
    part_r2, part_l2 = part(c + 2, cols), part(c - 2, cols)
    from_left, sum_r, sum_l, part_r2, part_l2, cols = hold((from_left, sum_r, sum_l, part_r2, part_l2, cols))
    sum_r, sum_l = z_shift(part_r2 + sum_r, 1), z_shift(part_l2 + sum_l, -1)
    part_r1, part_l1 = part(c + 1, cols), part(c - 1, cols)
    v = quarter(y) + from_left + from_right + across
    v, part_r1, part_l1 = hold((v, part_r1, part_l1))
    a, b, g = far_swap(v), x_swap(v[64:]), diagonal_swap(v[64:])
    a, b, g, sum_r, sum_l = hold((a, b, g, sum_r, sum_l))
    t = (v[64:] + b) + (a[64:] + g)
    t = t + z_xor(t, 1)
    sum_r, sum_l = part_r1 + sum_r, part_l1 + sum_l
    got = x_swap(cat(rows(sum_r, e * 256, 256), rows(sum_l, e * 256, 256)))
    t = t + z_xor(t, 2)
    t, got = hold((t + z_xor(t, 6), got))
    v = cat(v[:64] + a[:64], t)
    p1, m1, p2 = y_shift(v, -1), y_shift(v, 1), y_shift(v, 2)
    sum_r = z_shift(rows(sum_r, d * 256, 256) + got[:256], 1)
    sum_l = z_shift(rows(sum_l, d * 256, 256) + got[256:], -1)
    v, sum_r, sum_l = hold((cat(v, p1, p2, m1), sum_r, sum_l))
    part_0 = rows(part_0, d * 256, 256) + sum_0
    adj_rows, adj_cols, diag_adj = finish(
        core, y, v, core_swap(v), bar_cols, bar_diag, inv_diag, bar_rows - part_0, sum_r, sum_l
    )
    return adj_rows, adj_cols, diag_adj


def solution(mesh):
    in_specs = (
        P("row", ("col", "depth")),
        P(("row", "col", "depth"), None),
        P(("col", "depth"), None),
        P(("row", "col", "depth"), None),
        P(("col", "depth"), None),
        P(),
        P(),
    )
    out_specs = (P(("row", "col", "depth"), None), P(("col", "depth"), None), P())
    return jax.shard_map(body, mesh=mesh, in_specs=in_specs, out_specs=out_specs, check_vma=False)
```

```python
import functools

import jax
import jax.numpy as jnp
from jax import lax
from jax.experimental import pallas as pl
from jax.experimental.pallas import tpu as pltpu
from jax.sharding import PartitionSpec as P

HIGH = lax.Precision.HIGH
F32 = jnp.float32


def dot(a, b):
    return jnp.dot(a, b, precision=HIGH, preferred_element_type=F32)


def dot_t(a, b):
    return lax.dot_general(a, b, (((0,), (0,)), ((), ())), precision=HIGH, preferred_element_type=F32)


def split(a):
    top = a.astype(jnp.bfloat16)
    return top, (a - top.astype(F32)).astype(jnp.bfloat16)


def dot3(a, b, a_dim):
    dims = (((a_dim,), (0,)), ((), ()))
    a_top, a_low = split(a)
    b_top, b_low = split(b)
    one = functools.partial(lax.dot_general, dimension_numbers=dims, preferred_element_type=F32)
    return one(a_top, b_top) + (one(a_top, b_low) + one(a_low, b_top))


def finish_kernel(idx, mine, got, bar_cols, bar_diag, inv, adj_cols, diag_adj, cols, total):
    for half, core in ((mine, idx[0]), (got, 1 - idx[0])):
        for j in range(4):
            y = (idx[1] + j) & 3
            cols[pl.ds(pl.multiple_of(core * 256 + y * 64, 64), 64), :] = half[j * 96 : j * 96 + 64, :]
            total[pl.ds(pl.multiple_of(core * 128 + y * 32, 32), 32), :] = half[j * 96 + 64 : j * 96 + 96, :]
    diag_adj[...] = bar_diag[...] - dot3(inv[...], total[...], 0)
    adj_cols[...] = dot3(bar_cols[...] - cols[...], inv[...], 1)


def finish(core, y, mine, got, bar_cols, bar_diag, inv):
    vmem = pl.BlockSpec(memory_space=pltpu.VMEM)
    return pl.pallas_call(
        finish_kernel,
        out_shape=(jax.ShapeDtypeStruct((512, 256), F32), jax.ShapeDtypeStruct((256, 256), F32)),
        in_specs=[pl.BlockSpec(memory_space=pltpu.SMEM)] + [vmem] * 5,
        out_specs=(vmem, vmem),
        scratch_shapes=[pltpu.VMEM((512, 256), F32), pltpu.VMEM((256, 256), F32)],
        compiler_params=pltpu.CompilerParams(vmem_limit_bytes=8 * 1024 * 1024),
        cost_estimate=pl.CostEstimate(flops=400_000_000, bytes_accessed=3_000_000, transcendentals=0),
    )(jnp.stack([core, y]).astype(jnp.int32), mine, got, bar_cols, bar_diag, inv)


def rows(a, start, size):
    return lax.dynamic_slice_in_dim(a, start, size, 0)


def z_shift(a, k):
    return lax.ppermute(a, "col", [(i, (i + k) % 8) for i in range(8)])


def z_xor(a, k):
    return lax.ppermute(a, "col", [(i, i ^ k) for i in range(8)])


def z_shift_other(a, k):
    return lax.ppermute(a, ("col", "depth"), [(i, ((i >> 1) + k) % 8 * 2 + (1 - (i & 1))) for i in range(16)])


def x_swap(a):
    return lax.ppermute(a, "depth", [(0, 1), (1, 0)])


def core_swap(a):
    return lax.ppermute(a, "row", [(i, i ^ 1) for i in range(16)])


def far_swap(a):
    return lax.ppermute(a, "row", [(i, i ^ 8) for i in range(16)])


def diagonal_swap(a):
    return lax.ppermute(a, ("row", "depth"), [(i, i ^ 17) for i in range(32)])


def y_shift(a, k):
    return lax.ppermute(a, "row", [(i, (i & 9) | ((((i >> 1) + k) & 3) << 1)) for i in range(16)])


def body(slab_adj, panel_rows, panel_cols, bar_rows, bar_cols, inv_diag, bar_diag):
    r = lax.axis_index("row")
    c = lax.axis_index("col")
    d = lax.axis_index("depth")
    core, y, far = r & 1, (r >> 1) & 3, r >> 3

    cat = lambda *a: jnp.concatenate(a, 0)
    hold = lax.optimization_barrier
    e = 1 - d

    def slab(cc, dd):
        return rows(slab_adj, ((cc & 7) * 2 + dd) * 256, 256)

    def add(product, blk, cc, dd):
        return product + dot_t(slab(cc, dd), blk)

    def part(cc, cols):
        return dot(rows(slab_adj, (cc & 7) * 512, 512), cols)

    own = panel_rows
    right, left, other = z_shift(own, 1), z_shift(own, -1), x_swap(own)
    part_4 = part(c + 4, panel_cols)
    sum_r, sum_l = z_shift(part_4[:256], 1), z_shift(part_4[256:], -1)
    right, left, other, cols, own = hold((right, left, other, panel_cols, own))

    over_x = x_swap(cat(right[:128], left[:128]))
    to_right, to_left = z_shift(cat(right, other[128:]), 1), z_shift(cat(other[128:], left), -1)
    product = dot_t(slab(c, d), own)
    product = add(product, other, c, e)
    first_right, first_left = right, left
    right, left, over_x, product, first_right, first_left, sum_r, sum_l, cols = hold(
        (to_right, to_left, over_x, product, first_right, first_left, sum_r, sum_l, cols)
    )

    def add_own(product, k, right, left):
        return add(add(product, right, c - k, d), left, c + k, d)

    def add_other(product, k, over_x, right_b, left_b):
        product = add(product, cat(over_x[:128], right_b), c - k, e)
        return add(product, cat(over_x[128:], left_b), c + k, e)

    next_x = x_swap(cat(right[:128], left[128:256]))
    to_right, to_left = z_shift(right, 1), z_shift(left, -1)
    product = add_own(product, 1, first_right, first_left)
    product = add_own(product, 2, right[:256], left[128:])
    product = add_other(product, 1, over_x, right[256:], left[:128])
    part_r1, part_l1 = part(c + 1, cols), part(c - 1, cols)
    right, left, over_x, product, part_r1, part_l1, cols = hold(
        (to_right, to_left, next_x, product, part_r1, part_l1, cols)
    )

    next_x = x_swap(cat(right[:128], left[128:256]))
    to_right, to_left = z_shift(right[128:], 1), z_shift(left[:256], -1)
    from_right, from_left = z_shift_other(right[128:256], 1), z_shift_other(left[128:256], -1)
    product = add_own(product, 3, right[:256], left[128:])
    product = add_other(product, 2, over_x, right[256:], left[:128])
    part_r3, part_l3 = part(c + 3, cols), part(c - 3, cols)
    share = rows(bar_cols, r * 32, 32)
    share_cols = rows(cols, r * 32, 32)
    ahead = dot_t(cat(bar_rows, share), cat(panel_rows, share_cols))
    right, left, over_x, from_right, from_left, product, part_r3, part_l3, ahead, cols = hold(
        (to_right, to_left, next_x, from_right, from_left, product, part_r3, part_l3, ahead, cols)
    )
    sum_r = z_shift(cat(part_r3[:256] + sum_r, part_r3[256:]), 1)
    sum_l = z_shift(cat(part_l3[:256], part_l3[256:] + sum_l), -1)
    product = add(product, cat(left[128:256], right[:128]), c + 4, d)
    product = add(product, cat(from_left, from_right), c + 4, e)
    product = add_other(product, 3, over_x, right[128:256], left[:128])

    both = ahead - dot_t(cat(panel_cols, product), cat(product, panel_cols))

    def half(cc):
        return cat(rows(product, cc * 256, 256), rows(both, cc * 128, 128))

    v = half(core) + core_swap(half(1 - core))

    def quarter(yy):
        yy = yy & 3
        return cat(rows(v, yy * 64, 64), rows(v, 256 + yy * 32, 32))

    from_left, from_right, across = y_shift(quarter(y + 1), 1), y_shift(quarter(y - 1), -1), y_shift(quarter(y + 2), 2)
    part_r2, part_l2 = part(c + 2, cols), part(c - 2, cols)
    from_left, sum_r, sum_l, part_r2, part_l2, cols = hold((from_left, sum_r, sum_l, part_r2, part_l2, cols))
    sum_r, sum_l = z_shift(part_r2 + sum_r, 1), z_shift(part_l2 + sum_l, -1)
    part_0 = part(c, cols)
    v = quarter(y) + from_left + from_right + across
    v, part_0 = hold((v, part_0))
    a, b, g = far_swap(v), x_swap(v[64:]), diagonal_swap(v[64:])
    t = (v[64:] + b) + (a[64:] + g)
    t = t + z_xor(t, 1)
    t, sum_r, sum_l = hold((t, sum_r, sum_l))
    t = t + z_xor(t, 2)
    t, sum_r, sum_l = hold((t, sum_r, sum_l))
    sum_r, sum_l = z_shift(part_r1 + sum_r, 1), z_shift(part_l1 + sum_l, -1)
    t = t + z_xor(t, 6)
    v = cat(v[:64] + a[:64], t)
    p1, m1, p2 = y_shift(v, -1), y_shift(v, 1), y_shift(v, 2)
    p1, sum_r, sum_l = hold((p1, sum_r, sum_l))
    whole = part_0 + sum_r + sum_l
    over_x = x_swap(rows(whole, e * 256, 256))
    v = cat(v, p1, p2, m1)
    adj_cols, diag_adj = finish(core, y, v, core_swap(v), bar_cols, bar_diag, inv_diag)
    term_rows = rows(whole, d * 256, 256) + over_x
    adj_rows = dot(bar_rows - term_rows, inv_diag)
    return adj_rows, adj_cols, diag_adj


def solution(mesh):
    in_specs = (
        P("row", ("col", "depth")),
        P(("row", "col", "depth"), None),
        P(("col", "depth"), None),
        P(("row", "col", "depth"), None),
        P(("col", "depth"), None),
        P(),
        P(),
    )
    out_specs = (P(("row", "col", "depth"), None), P(("col", "depth"), None), P())
    return jax.shard_map(body, mesh=mesh, in_specs=in_specs, out_specs=out_specs, check_vma=False)
```

```python
import functools

import jax
import jax.numpy as jnp
from jax import lax
from jax.experimental import pallas as pl
from jax.experimental.pallas import tpu as pltpu
from jax.sharding import PartitionSpec as P

HIGH = lax.Precision.HIGH
F32 = jnp.float32


def dot(a, b):
    return jnp.dot(a, b, precision=HIGH, preferred_element_type=F32)


def dot_t(a, b):
    return lax.dot_general(a, b, (((0,), (0,)), ((), ())), precision=HIGH, preferred_element_type=F32)


def split(a):
    top = a.astype(jnp.bfloat16)
    return top, (a - top.astype(F32)).astype(jnp.bfloat16)


def dot3(a, b, a_dim):
    dims = (((a_dim,), (0,)), ((), ()))
    a_top, a_low = split(a)
    b_top, b_low = split(b)
    one = functools.partial(lax.dot_general, dimension_numbers=dims, preferred_element_type=F32)
    return one(a_top, b_top) + (one(a_top, b_low) + one(a_low, b_top))


def finish_kernel(
    idx, mine, got, bar_cols, bar_diag, inv, rest, over_x, adj_rows, adj_cols, diag_adj, cols, total
):
    adj_rows[...] = dot3(rest[...] - over_x[...], inv[...], 1)
    for half, core in ((mine, idx[0]), (got, 1 - idx[0])):
        for j in range(4):
            y = (idx[1] + j) & 3
            cols[pl.ds(pl.multiple_of(core * 256 + y * 64, 64), 64), :] = half[j * 96 : j * 96 + 64, :]
            total[pl.ds(pl.multiple_of(core * 128 + y * 32, 32), 32), :] = half[j * 96 + 64 : j * 96 + 96, :]
    diag_adj[...] = bar_diag[...] - dot3(inv[...], total[...], 0)
    adj_cols[...] = dot3(bar_cols[...] - cols[...], inv[...], 1)


def finish(core, y, mine, got, bar_cols, bar_diag, inv, rest, over_x):
    vmem = pl.BlockSpec(memory_space=pltpu.VMEM)
    return pl.pallas_call(
        finish_kernel,
        out_shape=tuple(jax.ShapeDtypeStruct((n, 256), F32) for n in (256, 512, 256)),
        in_specs=[pl.BlockSpec(memory_space=pltpu.SMEM)] + [vmem] * 7,
        out_specs=(vmem, vmem, vmem),
        scratch_shapes=[pltpu.VMEM((512, 256), F32), pltpu.VMEM((256, 256), F32)],
        compiler_params=pltpu.CompilerParams(vmem_limit_bytes=8 * 1024 * 1024),
        cost_estimate=pl.CostEstimate(flops=400_000_000, bytes_accessed=3_000_000, transcendentals=0),
    )(jnp.stack([core, y]).astype(jnp.int32), mine, got, bar_cols, bar_diag, inv, rest, over_x)


def rows(a, start, size):
    return lax.dynamic_slice_in_dim(a, start, size, 0)


def z_shift(a, k):
    return lax.ppermute(a, "col", [(i, (i + k) % 8) for i in range(8)])


def z_xor(a, k):
    return lax.ppermute(a, "col", [(i, i ^ k) for i in range(8)])


def z_shift_other(a, k):
    return lax.ppermute(a, ("col", "depth"), [(i, ((i >> 1) + k) % 8 * 2 + (1 - (i & 1))) for i in range(16)])


def x_swap(a):
    return lax.ppermute(a, "depth", [(0, 1), (1, 0)])


def core_swap(a):
    return lax.ppermute(a, "row", [(i, i ^ 1) for i in range(16)])


def far_swap(a):
    return lax.ppermute(a, "row", [(i, i ^ 8) for i in range(16)])


def diagonal_swap(a):
    return lax.ppermute(a, ("row", "depth"), [(i, i ^ 17) for i in range(32)])


def y_shift(a, k):
    return lax.ppermute(a, "row", [(i, (i & 9) | ((((i >> 1) + k) & 3) << 1)) for i in range(16)])


def body(slab_adj, panel_rows, panel_cols, bar_rows, bar_cols, inv_diag, bar_diag):
    r = lax.axis_index("row")
    c = lax.axis_index("col")
    d = lax.axis_index("depth")
    core, y, far = r & 1, (r >> 1) & 3, r >> 3

    cat = lambda *a: jnp.concatenate(a, 0)
    hold = lax.optimization_barrier
    e = 1 - d

    def slab(cc, dd):
        return rows(slab_adj, ((cc & 7) * 2 + dd) * 256, 256)

    def add(product, blk, cc, dd):
        return product + dot_t(slab(cc, dd), blk)

    def part(cc, cols):
        return dot(rows(slab_adj, (cc & 7) * 512, 512), cols)

    own = panel_rows
    right, left, other = z_shift(own, 1), z_shift(own, -1), x_swap(own)
    part_4 = part(c + 4, panel_cols)
    sum_r, sum_l = z_shift(part_4[:256], 1), z_shift(part_4[256:], -1)
    right, left, other, cols, own = hold((right, left, other, panel_cols, own))

    over_x = x_swap(cat(right[:128], left[:128]))
    to_right, to_left = z_shift(cat(right, other[128:]), 1), z_shift(cat(other[128:], left), -1)
    product = dot_t(slab(c, d), own)
    product = add(product, other, c, e)
    first_right, first_left = right, left
    right, left, over_x, product, first_right, first_left, sum_r, sum_l, cols = hold(
        (to_right, to_left, over_x, product, first_right, first_left, sum_r, sum_l, cols)
    )

    def add_own(product, k, right, left):
        return add(add(product, right, c - k, d), left, c + k, d)

    def add_other(product, k, over_x, right_b, left_b):
        product = add(product, cat(over_x[:128], right_b), c - k, e)
        return add(product, cat(over_x[128:], left_b), c + k, e)

    next_x = x_swap(cat(right[:128], left[128:256]))
    to_right, to_left = z_shift(right, 1), z_shift(left, -1)
    product = add_own(product, 1, first_right, first_left)
    product = add_own(product, 2, right[:256], left[128:])
    product = add_other(product, 1, over_x, right[256:], left[:128])
    part_r1, part_l1 = part(c + 1, cols), part(c - 1, cols)
    right, left, over_x, product, part_r1, part_l1, cols = hold(
        (to_right, to_left, next_x, product, part_r1, part_l1, cols)
    )

    next_x = x_swap(cat(right[:128], left[128:256]))
    to_right, to_left = z_shift(right[128:], 1), z_shift(left[:256], -1)
    from_right, from_left = z_shift_other(right[128:256], 1), z_shift_other(left[128:256], -1)
    product = add_own(product, 3, right[:256], left[128:])
    product = add_other(product, 2, over_x, right[256:], left[:128])
    part_r3, part_l3 = part(c + 3, cols), part(c - 3, cols)
    share = rows(bar_cols, r * 32, 32)
    share_cols = rows(cols, r * 32, 32)
    ahead = dot_t(cat(bar_rows, share), cat(panel_rows, share_cols))
    right, left, over_x, from_right, from_left, product, part_r3, part_l3, ahead, cols = hold(
        (to_right, to_left, next_x, from_right, from_left, product, part_r3, part_l3, ahead, cols)
    )
    sum_r = z_shift(cat(part_r3[:256] + sum_r, part_r3[256:]), 1)
    sum_l = z_shift(cat(part_l3[:256], part_l3[256:] + sum_l), -1)
    product = add(product, cat(left[128:256], right[:128]), c + 4, d)
    product = add(product, cat(from_left, from_right), c + 4, e)
    product = add_other(product, 3, over_x, right[128:256], left[:128])

    both = ahead - dot_t(cat(panel_cols, product), cat(product, panel_cols))

    def half(cc):
        return cat(rows(product, cc * 256, 256), rows(both, cc * 128, 128))

    v = half(core) + core_swap(half(1 - core))

    def quarter(yy):
        yy = yy & 3
        return cat(rows(v, yy * 64, 64), rows(v, 256 + yy * 32, 32))

    from_left, from_right, across = y_shift(quarter(y + 1), 1), y_shift(quarter(y - 1), -1), y_shift(quarter(y + 2), 2)
    part_r2, part_l2 = part(c + 2, cols), part(c - 2, cols)
    from_left, sum_r, sum_l, part_r2, part_l2, cols = hold((from_left, sum_r, sum_l, part_r2, part_l2, cols))
    sum_r, sum_l = z_shift(part_r2 + sum_r, 1), z_shift(part_l2 + sum_l, -1)
    part_0 = part(c, cols)
    v = quarter(y) + from_left + from_right + across
    v, part_0 = hold((v, part_0))
    a, b, g = far_swap(v), x_swap(v[64:]), diagonal_swap(v[64:])
    t = (v[64:] + b) + (a[64:] + g)
    t = t + z_xor(t, 1)
    t, sum_r, sum_l = hold((t, sum_r, sum_l))
    t = t + z_xor(t, 2)
    t = t + z_xor(t, 6)
    t, sum_r, sum_l = hold((t, part_r1 + sum_r, part_l1 + sum_l))
    sum_r, sum_l = z_shift(sum_r, 1), z_shift(sum_l, -1)
    v = cat(v[:64] + a[:64], t)
    p1, m1, p2 = y_shift(v, -1), y_shift(v, 1), y_shift(v, 2)
    p1, sum_r, sum_l = hold((p1, sum_r, sum_l))
    whole = part_0 + sum_r + sum_l
    over_x = x_swap(rows(whole, e * 256, 256))
    v = cat(v, p1, p2, m1)
    rest = bar_rows - rows(whole, d * 256, 256)
    adj_rows, adj_cols, diag_adj = finish(
        core, y, v, core_swap(v), bar_cols, bar_diag, inv_diag, rest, over_x
    )
    return adj_rows, adj_cols, diag_adj


def solution(mesh):
    in_specs = (
        P("row", ("col", "depth")),
        P(("row", "col", "depth"), None),
        P(("col", "depth"), None),
        P(("row", "col", "depth"), None),
        P(("col", "depth"), None),
        P(),
        P(),
    )
    out_specs = (P(("row", "col", "depth"), None), P(("col", "depth"), None), P())
    return jax.shard_map(body, mesh=mesh, in_specs=in_specs, out_specs=out_specs, check_vma=False)
```
